256 devices in a mesh: section: 2 (over core), blk: 16 (over y_hi, z), head: 8 (over y_lo, x).
Axes of the slice: x: 4, y: 4 (y_hi: 2, y_lo: 2; y = y_hi * 2 + y_lo), z: 8, core: 2. Of those that a mesh axis runs over, the one named last changes fastest.
Arguments:
- projected: bfloat16 [16384, 8192], P(('section', 'blk')), may hold values from -6 to 6
- key_weight: bfloat16 [8192, 1024], P(None, 'head'), may hold values from -0.0625 to 0.0625
- value_weight: bfloat16 [8192, 1024], P(None, 'head'), may hold values from -0.0625 to 0.0625
- key_gain: float32 [128], replicated, may hold values from 0.1 to 1.9
- queries: bfloat16 [2048, 8, 1024], P('blk', 'section', 'head'), may hold values from -320 to 320
- frame_tokens: int32 [32], replicated, may hold values from 1 to 1024, 16384 in all
- span_first: int32 [2048], replicated, may hold values from 0 to 31
- span_count: int32 [2048], replicated, may hold values from 1 to 32
Outputs:
- attended: bfloat16 [2048, 8, 1024], P('blk', 'section', 'head')
The draws below stay inside these ranges and needn't reach their ends.
Inputs may be any that keep to these rules, and one draw needn't show every extreme that they name: Frame f holds frame_tokens[f] consecutive visual tokens, and they sum to 16384.
All inputs are finite; a program needn't handle non-finite values.
Results may differ from the reference program's by a relative error of at most 0.005.
The reference program's roundings to bfloat16 on the way count: a program that leaves them out, or rounds other values in their place, can miss the bound.
Values may be sent and summed in bfloat16 or wider, within the bound.
A program may use at most 128 MiB of HBM per device.

```python
import math
import jax
import jax.numpy as jnp
import numpy as np
from jax import lax

D = 8192
KV = 8
QPG = 8
HD = 128
FRAMES = 32
VT = 16384
QTOT = 2048
FMAX = 1024


def draw_queries(key, part):
    normal_part = jax.random.normal(jax.random.fold_in(key, 11), (QTOT, QPG, KV * HD), jnp.float32)
    normal_part = jnp.clip(normal_part, -5.0, 5.0)
    return (normal_part * 2.5).astype(jnp.bfloat16)


def with_ends(values, own_key, low, high):
    dims = values.shape
    place = [jax.random.randint(jax.random.fold_in(own_key, axis), (), 0, dims[axis]) for axis in range(len(dims))]
    values = values.at[tuple(place)].set(low)
    longest = dims.index(max(dims))
    place[longest] = (place[longest] + 1) % dims[longest]
    return values.at[tuple(place)].set(high)


def shard_levels(stream_key, dims, shards, low, high):
    gain = 1.0
    for position, blocks in shards:
        steps = jax.random.uniform(jax.random.fold_in(jax.random.fold_in(stream_key, 6), position), (blocks,), jnp.float32, low / len(shards), high / len(shards))
        gain = gain * jnp.repeat(jnp.exp(steps), dims[position] // blocks).reshape((-1,) + (1,) * (len(dims) - 1 - position))
    return gain


def split_up(count, total, bound, slope):
    portions = [(1 << 20) // math.isqrt(rank ** slope) + 1 for rank in range(2, count + 1)]
    spare, counts = total - bound - (count - 1), [1] * (count - 1)
    while spare > 0:
        candidates = [i for i in range(count - 1) if counts[i] < bound]
        mass, budget = sum([portions[i] for i in candidates]), spare
        for i in candidates:
            addition = min(bound - counts[i], max(1, budget * portions[i] // mass), spare)
            counts[i] = counts[i] + addition
            spare = spare - addition
    return np.array([bound] + counts)


def uneven(own_key, count, total, reach, skew):
    if count == 2:
        one = jax.random.randint(own_key, (), max(1, total - reach), min(reach, total - 1) + 1)
        return jnp.stack([one, total - one])
    lengths = jnp.asarray(split_up(count, total, reach, skew), jnp.int32)
    couples = (count - 1) // 2
    source_of, sink = lengths[1:1 + 2 * couples:2], lengths[2:2 + 2 * couples:2]
    margin = jnp.minimum(source_of - 1, reach - sink)
    shifted = jax.random.randint(jax.random.fold_in(own_key, 1), (couples,), 0, 1 << 20) % (margin + 1)
    lengths = lengths.at[1:1 + 2 * couples:2].set(source_of - shifted).at[2:2 + 2 * couples:2].set(sink + shifted)
    return lengths[jax.random.permutation(jax.random.fold_in(own_key, 2), count)]


def gaussian(key, shape, deviation, reach, cuts=(), held_as=jnp.bfloat16):
    level = shard_levels(key, shape, cuts, -0.22, 0.18) if cuts else 1.0
    entries = jax.random.normal(key, shape, jnp.float32) * deviation * level
    return jnp.minimum(jnp.maximum(entries, -reach), reach).astype(held_as)


def setup_inputs(seed: int = 0) -> dict:
    streams_of = jax.random.split(jax.random.key(seed), 9)
    return {
        "projected": gaussian(streams_of[0], (VT, D), 1.0, 6.0, ((0, 32),)),
        "key_weight": gaussian(streams_of[1], (D, KV * HD), D ** -0.5, 0.0625, ((1, 8),)),
        "value_weight": gaussian(streams_of[2], (D, KV * HD), D ** -0.5, 0.0625, ((1, 8),)),
        "key_gain": jnp.clip(1.0 + 0.18 * jax.random.normal(streams_of[3], (HD,), jnp.float32), 0.1, 1.9),
        "queries": draw_queries(jax.random.fold_in(streams_of[8], 71), 0),
        "frame_tokens": uneven(streams_of[5], FRAMES, VT, FMAX, 1).astype(jnp.int32),
        "span_first": with_ends(jax.random.randint(streams_of[6], (QTOT,), 0, FRAMES), jax.random.fold_in(streams_of[6], 1), 0, FRAMES - 1).astype(jnp.int32),
        "span_count": with_ends(jax.random.randint(streams_of[7], (QTOT,), 1, FRAMES + 1), jax.random.fold_in(streams_of[7], 1), 1, FRAMES).astype(jnp.int32),
    }


def span_bounds(frame_tokens, span_first, span_count):
    frame_ids = jnp.arange(FRAMES, dtype=jnp.int32)
    span_end = jnp.minimum(span_first + span_count, FRAMES)
    first_token = lax.optimization_barrier(jnp.sum(jnp.where(frame_ids[None, :] < span_first[:, None], frame_tokens[None, :], 0), axis=1)).astype(jnp.int32)
    end_token = lax.optimization_barrier(jnp.sum(jnp.where(frame_ids[None, :] < span_end[:, None], frame_tokens[None, :], 0), axis=1)).astype(jnp.int32)
    return (first_token, end_token)

def reference(projected, key_weight, value_weight, key_gain, queries, frame_tokens, span_first, span_count):
    key_raw = jnp.dot(projected, key_weight, preferred_element_type=jnp.float32).reshape(VT, KV, HD)
    mean_square = lax.optimization_barrier(jnp.mean(key_raw * key_raw, axis=2, keepdims=True))
    key_table = (key_raw / jnp.sqrt(mean_square + 1e-05) * key_gain).astype(jnp.bfloat16)
    value_table = jnp.dot(projected, value_weight, preferred_element_type=jnp.float32).astype(jnp.bfloat16).reshape(VT, KV, HD)
    key_table = lax.optimization_barrier(key_table)
    value_table = lax.optimization_barrier(value_table)
    first_token, end_token = span_bounds(frame_tokens, span_first, span_count)
    positions = jnp.arange(VT, dtype=jnp.int32)
    block_rows = math.gcd(QTOT, 128)
    block_count = QTOT // block_rows
    keys_by_head = jnp.transpose(key_table, (1, 0, 2)).astype(jnp.float32)
    values_by_head = jnp.transpose(value_table, (1, 0, 2)).astype(jnp.float32)
    queries_by_head = jnp.transpose(queries.reshape(QTOT, QPG, KV, HD), (2, 0, 1, 3)).astype(jnp.float32)
    first_blocks = first_token.reshape(block_count, block_rows)
    end_blocks = end_token.reshape(block_count, block_rows)

    def per_head(operands):
        head_queries, head_keys, head_values = operands

        def per_block(block_operands):
            block_queries, block_first, block_end = block_operands
            scores = jnp.einsum('npd,md->npm', block_queries, head_keys) * HD ** (-0.5)
            allowed = (positions[None, :] >= block_first[:, None]) & (positions[None, :] < block_end[:, None])
            scores = jnp.where(allowed[:, None, :], scores, -1e+30)
            row_max = lax.optimization_barrier(jnp.max(scores, axis=2, keepdims=True))
            weights = jnp.exp(scores - row_max)
            denominator = lax.optimization_barrier(jnp.sum(weights, axis=2))
            rounded = lax.optimization_barrier(weights.astype(jnp.bfloat16)).astype(jnp.float32)
            numerator = jnp.einsum('npm,md->npd', rounded, head_values)
            return numerator / denominator[:, :, None]
        blocks = lax.map(per_block, (head_queries.reshape(block_count, block_rows, QPG, HD), first_blocks, end_blocks))
        return blocks.reshape(QTOT, QPG, HD)
    attended = lax.map(per_head, (queries_by_head, keys_by_head, values_by_head))
    return jnp.transpose(attended, (1, 2, 0, 3)).reshape(QTOT, QPG, KV * HD).astype(jnp.bfloat16)
```

```python
import functools
import math

import jax
import jax.numpy as jnp
from jax import lax
from jax.experimental import pallas as pl
from jax.experimental.pallas import tpu as pltpu
from jax.sharding import PartitionSpec as P

HD = 128
FRAMES = 32
Z = 8
NEG = -1e30
SCALE = math.log2(math.e) / math.sqrt(HD)
EPS = 1e-05
ROW_TILE = 256
DEPTH = 1024
MESH = pl.DeviceIdType.MESH
f32 = jnp.float32
bf16 = jnp.bfloat16


def nt_dot(a, b):
    return lax.dot_general(a, b, (((1,), (1,)), ((), ())), preferred_element_type=f32)


def kernel(
    x_hbm, kw_hbm, vw_hbm, gain_ref, q_hbm, frames_ref, first_ref, count_ref,
    out_ref,
    xb, wb, raw, kv, kvs, qb, feat, ka, va, m_ref, acc_ref, o_send, o_recv, l_send, l_recv,
    in_sem, q_sem, r_send, r_recv, s_send, s_recv, qx_sem, ox_sem,
):
    steps = xb.shape[0]
    rows = qb.shape[1]
    part = kv.shape[2]
    sec = lax.axis_index("section")
    blk = lax.axis_index("blk")
    head = lax.axis_index("head")
    y_hi = blk // Z
    z = lax.rem(blk, Z)
    partner_blk = (1 - y_hi) * Z + z
    right = (sec, y_hi * Z + lax.rem(z + 1, Z), head)
    left = (sec, y_hi * Z + lax.rem(z + Z - 1, Z), head)
    partner = (sec, partner_blk, head)
    sibling = (1 - sec, blk, head)

    def in_copies(i):
        at = pl.ds(i * DEPTH, DEPTH)
        return (
            pltpu.make_async_copy(kw_hbm.at[at, :], wb.at[i, :, pl.ds(0, HD)], in_sem.at[0, i]),
            pltpu.make_async_copy(vw_hbm.at[at, :], wb.at[i, :, pl.ds(HD, HD)], in_sem.at[1, i]),
            pltpu.make_async_copy(x_hbm.at[:, at], xb.at[i], in_sem.at[2, i]),
        )

    own_q = pltpu.make_async_copy(q_hbm, qb.at[1], q_sem.at[0])
    own_q.start()
    for i in range(steps):
        for copy in in_copies(i):
            copy.start()

    barrier = pltpu.get_barrier_semaphore()
    for other in (right, left, partner, sibling):
        pl.semaphore_signal(barrier, inc=1, device_id=other, device_id_type=MESH)
    pl.semaphore_wait(barrier, 4)

    own_q.wait()
    q_copy = pltpu.make_async_remote_copy(
        src_ref=qb.at[1], dst_ref=qb.at[0], send_sem=qx_sem.at[0], recv_sem=qx_sem.at[1],
        device_id=partner, device_id_type=MESH,
    )
    q_copy.start()

    lane = lax.broadcasted_iota(jnp.int32, (1, HD), 1)
    starts = jnp.zeros((1, HD), jnp.int32)
    ends = jnp.zeros((1, HD), jnp.int32)
    for f in range(FRAMES):
        tokens = frames_ref[f]
        starts = starts + jnp.where(lane > f, tokens, 0)
        ends = ends + jnp.where(lane >= f, tokens, 0)
    ends = jnp.where(lane < FRAMES, ends, 0)
    heads_per_row = rows // first_ref.shape[1]
    text = first_ref.shape[1]
    spread = (
        lax.broadcasted_iota(jnp.int32, (rows, text), 0) // heads_per_row
        == lax.broadcasted_iota(jnp.int32, (rows, text), 1)
    ).astype(bf16)
    frame_id = lax.broadcasted_iota(jnp.int32, (HD, text), 0)
    for i, b in ((0, partner_blk), (1, blk)):
        first = first_ref[pl.ds(b, 1), :]
        end = jnp.minimum(first + count_ref[pl.ds(b, 1), :], FRAMES)
        closed = jnp.where((frame_id >= first) & (frame_id < end), 0.0, NEG).astype(bf16)
        feat[i] = nt_dot(spread, closed).astype(bf16)

    m_ref[...] = jnp.full_like(m_ref, 2 * NEG)
    acc_ref[...] = jnp.zeros_like(acc_ref)
    va[:, HD:] = jnp.ones_like(va[:, HD:])

    raw[...] = jnp.zeros_like(raw)

    def project(i, carry):
        for copy in in_copies(i):
            copy.wait()
        raw[...] += jnp.dot(xb[i], wb[i], preferred_element_type=f32)
        return carry

    lax.fori_loop(0, steps, project, 0)
    key_raw = raw[:, :HD]
    mean_square = jnp.mean(key_raw * key_raw, axis=1, keepdims=True)
    keys = (key_raw / jnp.sqrt(mean_square + EPS) * gain_ref[...]).astype(bf16)
    values = raw[:, HD:].astype(bf16)
    for j in range(2):
        kv[0, j, :, :HD] = keys[j * part : (j + 1) * part]
        kv[0, j, :, HD:] = values[j * part : (j + 1) * part]

    def ring_copy(direction, k, source):
        return pltpu.make_async_remote_copy(
            src_ref=source, dst_ref=kv.at[k + 1, direction],
            send_sem=r_send.at[direction, k], recv_sem=r_recv.at[direction, k],
            device_id=(right, left)[direction], device_id_type=MESH,
        )

    def to_sibling(e):
        return pltpu.make_async_remote_copy(
            src_ref=kv.at[e], dst_ref=kvs.at[e], send_sem=s_send.at[e], recv_sem=s_recv.at[e],
            device_id=sibling, device_id_type=MESH,
        )

    for k in range(2):
        ring_copy(0, k, kv.at[0, k]).start()
        ring_copy(1, k, kv.at[0, 1 - k]).start()
    to_sibling(0).start()

    def token_base(e, direction, section):
        hop = (e + 1) // 2
        if direction == 0:
            source, half = lax.rem(z + Z - hop, Z), lax.rem(e + 1, 2)
        else:
            source, half = lax.rem(z + hop, Z), lax.rem(e, 2)
        return ((section * 2 + y_hi) * Z + source) * (2 * part) + half * part

    def own_base(half, section):
        return ((section * 2 + y_hi) * Z + z) * (2 * part) + half * part

    def stage(slot, chunk, base):
        at = pl.ds(slot * part, part)
        pos = base + lax.broadcasted_iota(jnp.int32, (part, HD), 0)
        ka[at, :HD] = chunk[:, :HD]
        ka[at, HD:] = ((pos >= starts) & (pos < ends)).astype(bf16)
        va[at, :HD] = chunk[:, HD:]

    def attend(i, r, count):
        at = pl.ds(r * ROW_TILE, ROW_TILE)
        q = jnp.concatenate([qb[i, at, :], feat[i, at, :]], axis=1)
        k_all = ka[: count * part]
        v_all = va[: count * part]
        s = nt_dot(q, k_all)
        m_old = m_ref[i, at, :]
        m_new = jnp.maximum(m_old, jnp.max(s, axis=1, keepdims=True))
        p = jnp.exp2((s - m_new[:, :1]) * SCALE).astype(bf16)
        fade = jnp.exp2((m_old - m_new) * SCALE)
        m_ref[i, at, :] = m_new
        pv = jnp.dot(p, v_all, preferred_element_type=f32)
        acc_ref[i, at, :] = acc_ref[i, at, :] * jnp.concatenate([fade, fade], axis=1) + pv

    tiles = rows // ROW_TILE
    for j in range(2):
        stage(j, kv[0, j], own_base(j, sec))
    for r in range(tiles):
        attend(1, r, 2)
    q_copy.wait()
    for r in range(tiles):
        attend(0, r, 2)

    def arrivals(e, forward):
        for direction in range(2):
            ring_copy(direction, e - 1, kv.at[e, direction]).wait_recv()
            if forward:
                ring_copy(direction, e + 1, kv.at[e, direction]).start()
        to_sibling(e).start()
        to_sibling(e - 1).wait_recv()
        for direction in range(2):
            stage(direction, kv[e, direction], token_base(e, direction, sec))

    to_attend = [(i, r) for i in range(2) for r in range(tiles)]

    arrivals(1, True)
    for j in range(2):
        stage(2 + j, kvs[0, j], own_base(j, 1 - sec))
    for i, r in to_attend:
        attend(i, r, 4)

    def body(e, forward):
        arrivals(e, forward)
        for direction in range(2):
            stage(2 + direction, kvs[e - 1, direction], token_base(e - 1, direction, 1 - sec))
        for i, r in to_attend:
            attend(i, r, 4)

    def forwarding(e, carry):
        body(e, True)
        return carry

    def ending(e, carry):
        body(e, False)
        return carry

    lax.fori_loop(2, 6, forwarding, 0)
    lax.fori_loop(6, 8, ending, 0)

    to_sibling(7).wait_recv()
    for direction in range(2):
        stage(direction, kvs[7, direction], token_base(7, direction, 1 - sec))

    def o_copies(r):
        at = pl.ds(r * ROW_TILE, ROW_TILE)
        return (
            pltpu.make_async_remote_copy(
                src_ref=o_send.at[at, :], dst_ref=o_recv.at[at, :],
                send_sem=ox_sem.at[0, r], recv_sem=ox_sem.at[1, r],
                device_id=partner, device_id_type=MESH,
            ),
            pltpu.make_async_remote_copy(
                src_ref=l_send.at[r], dst_ref=l_recv.at[r],
                send_sem=ox_sem.at[2, r], recv_sem=ox_sem.at[3, r],
                device_id=partner, device_id_type=MESH,
            ),
        )

    def level(i, at):
        return m_ref[i, at, :] * SCALE + jnp.log2(acc_ref[i, at, HD:])

    for r in range(tiles):
        at = pl.ds(r * ROW_TILE, ROW_TILE)
        attend(0, r, 2)
        o_send[at, :] = (acc_ref[0, at, :HD] / acc_ref[0, at, HD:]).astype(bf16)
        weight = level(0, at)
        for h in range(ROW_TILE // HD):
            l_send[r, pl.ds(8 * h, 8), :] = weight[h * HD : (h + 1) * HD].T[:8]
        for copy in o_copies(r):
            copy.start()
    for r in range(tiles):
        attend(1, r, 2)
    for r in range(tiles):
        at = pl.ds(r * ROW_TILE, ROW_TILE)
        for copy in o_copies(r):
            copy.wait_recv()
        mine = level(1, at)
        theirs = jnp.concatenate(
            [
                jnp.broadcast_to(l_recv[r, 8 * h : 8 * h + 1, :], (HD, HD)).T
                for h in range(ROW_TILE // HD)
            ],
            axis=0,
        )
        top = jnp.maximum(mine, theirs)
        mine = jnp.exp2(mine - top)
        theirs = jnp.exp2(theirs - top)
        own = acc_ref[1, at, :HD] / acc_ref[1, at, HD:]
        total = (mine * own + theirs * o_recv[at, :].astype(f32)) / (mine + theirs)
        out_ref[at, :] = total.astype(bf16)

    for k in range(7):
        for direction in range(2):
            ring_copy(direction, k, kv.at[0, 0]).wait_send()
    for e in range(8):
        to_sibling(e).wait_send()
    for r in range(tiles):
        for copy in o_copies(r):
            copy.wait_send()


def body(
    projected, key_weight, value_weight, key_gain, queries, frame_tokens, span_first, span_count
):
    count, width = projected.shape
    text, sub_heads, _ = queries.shape
    rows = text * sub_heads
    part = count // 2
    steps = width // DEPTH
    anywhere = pl.BlockSpec(memory_space=pl.ANY)
    vmem = pl.BlockSpec(memory_space=pltpu.VMEM)
    out = pl.pallas_call(
        kernel,
        out_shape=jax.ShapeDtypeStruct((rows, HD), bf16),
        in_specs=[
            anywhere, anywhere, anywhere, vmem, anywhere,
            pl.BlockSpec(memory_space=pltpu.SMEM), vmem, vmem,
        ],
        out_specs=vmem,
        scratch_shapes=[
            pltpu.VMEM((steps, count, DEPTH), bf16),
            pltpu.VMEM((steps, DEPTH, 2 * HD), bf16),
            pltpu.VMEM((count, 2 * HD), f32),
            pltpu.VMEM((8, 2, part, 2 * HD), bf16),
            pltpu.VMEM((8, 2, part, 2 * HD), bf16),
            pltpu.VMEM((2, rows, HD), bf16),
            pltpu.VMEM((2, rows, HD), bf16),
            pltpu.VMEM((4 * part, 2 * HD), bf16),
            pltpu.VMEM((4 * part, 2 * HD), bf16),
            pltpu.VMEM((2, rows, HD), f32),
            pltpu.VMEM((2, rows, 2 * HD), f32),
            pltpu.VMEM((rows, HD), bf16),
            pltpu.VMEM((rows, HD), bf16),
            pltpu.VMEM((rows // ROW_TILE, 8 * (ROW_TILE // HD), HD), f32),
            pltpu.VMEM((rows // ROW_TILE, 8 * (ROW_TILE // HD), HD), f32),
            pltpu.SemaphoreType.DMA((3, steps)),
            pltpu.SemaphoreType.DMA((1,)),
            pltpu.SemaphoreType.DMA((2, 7)),
            pltpu.SemaphoreType.DMA((2, 7)),
            pltpu.SemaphoreType.DMA((8,)),
            pltpu.SemaphoreType.DMA((8,)),
            pltpu.SemaphoreType.DMA((2,)),
            pltpu.SemaphoreType.DMA((4, rows // ROW_TILE)),
        ],
        compiler_params=pltpu.CompilerParams(
            collective_id=0, has_side_effects=True, vmem_limit_bytes=50 * 2**20
        ),
        name="gather_attend",
    )(
        projected, key_weight, value_weight, key_gain.reshape(1, HD),
        queries.reshape(rows, HD), frame_tokens,
        span_first.reshape(-1, text), span_count.reshape(-1, text),
    )
    return out.reshape(text, sub_heads, HD)


def solution(mesh):
    placed = (
        P(("section", "blk"), None),
        P(None, "head"),
        P(None, "head"),
        P(),
        P("blk", "section", "head"),
        P(),
        P(),
        P(),
    )
    return jax.shard_map(
        body, mesh=mesh, in_specs=placed, out_specs=P("blk", "section", "head"), check_vma=False
    )
```

```python
import functools
import math

import jax
import jax.numpy as jnp
from jax import lax
from jax.experimental import pallas as pl
from jax.experimental.pallas import tpu as pltpu
from jax.sharding import PartitionSpec as P

HD = 128
FRAMES = 32
Z = 8
NEG = -1e30
SCALE = math.log2(math.e) / math.sqrt(HD)
EPS = 1e-05
ROW_TILE = 256
DEPTH = 1024
MESH = pl.DeviceIdType.MESH
f32 = jnp.float32
bf16 = jnp.bfloat16


def nt_dot(a, b):
    return lax.dot_general(a, b, (((1,), (1,)), ((), ())), preferred_element_type=f32)


def kernel(
    x_hbm, kw_hbm, vw_hbm, gain_hbm, q_hbm, frames_hbm, first_hbm, count_hbm,
    out_ref,
    gain_ref, frames_ref, first_ref, count_ref, xb, wb, kv, kvs, qb, feat, ka, va, m_ref, acc_ref, o_send, o_recv, l_send, l_recv,
    in_sem, q_sem, r_send, r_recv, s_send, s_recv, qx_sem, ox_sem,
):
    steps = xb.shape[1]
    rows = qb.shape[1]
    part = kv.shape[2]
    sec = lax.axis_index("section")
    blk = lax.axis_index("blk")
    head = lax.axis_index("head")
    y_hi = blk // Z
    z = lax.rem(blk, Z)
    partner_blk = (1 - y_hi) * Z + z
    right = (sec, y_hi * Z + lax.rem(z + 1, Z), head)
    left = (sec, y_hi * Z + lax.rem(z + Z - 1, Z), head)
    partner = (sec, partner_blk, head)
    sibling = (1 - sec, blk, head)

    def weight_copies(i):
        at = pl.ds(i * DEPTH, DEPTH)
        return (
            pltpu.make_async_copy(kw_hbm.at[at, :], wb.at[i, :, pl.ds(0, HD)], in_sem.at[0, i]),
            pltpu.make_async_copy(vw_hbm.at[at, :], wb.at[i, :, pl.ds(HD, HD)], in_sem.at[1, i]),
        )

    def row_copy(c, i):
        at = pl.ds(i * DEPTH, DEPTH)
        return pltpu.make_async_copy(
            x_hbm.at[pl.ds(2 * c * part, 2 * part), at], xb.at[c, i], in_sem.at[2 + c, i]
        )

    barrier = pltpu.get_barrier_semaphore()
    for other in (right, left, partner, sibling):
        pl.semaphore_signal(barrier, inc=1, device_id=other, device_id_type=MESH)

    for i in range(steps):
        for copy in weight_copies(i):
            copy.start()
        row_copy(0, i).start()
    own_q = pltpu.make_async_copy(q_hbm, qb.at[1], q_sem.at[0])
    own_q.start()
    small = [
        pltpu.make_async_copy(source, target, q_sem.at[1 + i])
        for i, (source, target) in enumerate(
            (
                (frames_hbm, frames_ref),
                (first_hbm, first_ref),
                (count_hbm, count_ref),
                (gain_hbm, gain_ref),
            )
        )
    ]
    for copy in small:
        copy.start()
    for i in range(steps):
        row_copy(1, i).start()

    def ring_copy(direction, k, source):
        return pltpu.make_async_remote_copy(
            src_ref=source, dst_ref=kv.at[1 + k // 2, 2 * (k % 2) + direction],
            send_sem=r_send.at[direction, k], recv_sem=r_recv.at[direction, k],
            device_id=(right, left)[direction], device_id_type=MESH,
        )

    def to_sibling(s):
        return pltpu.make_async_remote_copy(
            src_ref=kv.at[s], dst_ref=kvs.at[s], send_sem=s_send.at[s], recv_sem=s_recv.at[s],
            device_id=sibling, device_id_type=MESH,
        )

    q_copy = pltpu.make_async_remote_copy(
        src_ref=qb.at[1], dst_ref=qb.at[0], send_sem=qx_sem.at[0], recv_sem=qx_sem.at[1],
        device_id=partner, device_id_type=MESH,
    )
    for c in range(2):
        total = None
        for i in range(steps):
            if c == 0:
                for copy in weight_copies(i):
                    copy.wait()
            row_copy(c, i).wait()
            term = jnp.dot(xb[c, i], wb[i], preferred_element_type=f32)
            total = term if total is None else total + term
        if c == 0:
            for copy in small:
                copy.wait()
        key_raw = total[:, :HD]
        mean_square = jnp.mean(key_raw * key_raw, axis=1, keepdims=True)
        keys = (key_raw / jnp.sqrt(mean_square + EPS) * gain_ref[...]).astype(bf16)
        values = total[:, HD:].astype(bf16)
        for j in range(2):
            kv[0, 2 * c + j, :, :HD] = keys[j * part : (j + 1) * part]
            kv[0, 2 * c + j, :, HD:] = values[j * part : (j + 1) * part]
        if c == 0:
            pl.semaphore_wait(barrier, 4)
        ring_copy(0, c, kv.at[0, 2 * c]).start()
        ring_copy(1, c, kv.at[0, 2 * c + 1]).start()
        if c == 0:
            own_q.wait()
            q_copy.start()
    for c in range(2):
        ring_copy(0, 2 + c, kv.at[0, 2 * c + 1]).start()
        ring_copy(1, 2 + c, kv.at[0, 2 * c]).start()
    to_sibling(0).start()

    lane = lax.broadcasted_iota(jnp.int32, (1, HD), 1)
    starts = jnp.zeros((1, HD), jnp.int32)
    ends = jnp.zeros((1, HD), jnp.int32)
    for f in range(FRAMES):
        tokens = frames_ref[f]
        starts = starts + jnp.where(lane > f, tokens, 0)
        ends = ends + jnp.where(lane >= f, tokens, 0)
    ends = jnp.where(lane < FRAMES, ends, 0)
    heads_per_row = rows // first_ref.shape[1]
    text = first_ref.shape[1]
    spread = (
        lax.broadcasted_iota(jnp.int32, (rows, text), 0) // heads_per_row
        == lax.broadcasted_iota(jnp.int32, (rows, text), 1)
    ).astype(bf16)
    frame_id = lax.broadcasted_iota(jnp.int32, (HD, text), 0)
    for i, b in ((0, partner_blk), (1, blk)):
        first = first_ref[pl.ds(b, 1), :]
        end = jnp.minimum(first + count_ref[pl.ds(b, 1), :], FRAMES)
        closed = jnp.where((frame_id >= first) & (frame_id < end), 0.0, NEG).astype(bf16)
        feat[i] = nt_dot(spread, closed).astype(bf16)

    m_ref[...] = jnp.full_like(m_ref, 2 * NEG)
    acc_ref[...] = jnp.zeros_like(acc_ref)
    va[:, HD:] = jnp.ones_like(va[:, HD:])

    def token_base(s, sub, direction, section):
        hop = (s + 1) // 2
        odd = lax.rem(s + 1, 2)
        if direction == 0:
            source, quarter = lax.rem(z + Z - hop, Z), odd + 2 * sub
        else:
            source, quarter = lax.rem(z + hop, Z), 1 - odd + 2 * sub
        return (((section * 2 + y_hi) * Z + source) * 4 + quarter) * part

    def own_base(quarter, section):
        return (((section * 2 + y_hi) * Z + z) * 4 + quarter) * part

    def stage(slot, chunk, base):
        at = pl.ds(slot * part, part)
        pos = base + lax.broadcasted_iota(jnp.int32, (part, HD), 0)
        ka[at, :HD] = chunk[:, :HD]
        ka[at, HD:] = ((pos >= starts) & (pos < ends)).astype(bf16)
        va[at, :HD] = chunk[:, HD:]

    def attend(i, r, slot, count):
        at = pl.ds(r * ROW_TILE, ROW_TILE)
        q = jnp.concatenate([qb[i, at, :], feat[i, at, :]], axis=1)
        keys_at = pl.ds(slot * part, count * part)
        k_all = ka[keys_at, :]
        v_all = va[keys_at, :]
        s = nt_dot(q, k_all)
        m_old = m_ref[i, at, :]
        m_new = jnp.maximum(m_old, jnp.max(s, axis=1, keepdims=True))
        p = jnp.exp2((s - m_new[:, :1]) * SCALE).astype(bf16)
        fade = jnp.exp2((m_old - m_new) * SCALE)
        m_ref[i, at, :] = m_new
        pv = jnp.dot(p, v_all, preferred_element_type=f32)
        acc_ref[i, at, :] = acc_ref[i, at, :] * jnp.concatenate([fade, fade], axis=1) + pv

    tiles = rows // ROW_TILE
    for j in range(4):
        stage(j, kv[0, j], own_base(j, sec))
    for r in range(tiles):
        attend(1, r, 0, 4)
    q_copy.wait()
    for r in range(tiles):
        attend(0, r, 0, 4)

    def arrivals(s, forward):
        for sub in range(2):
            for direction in range(2):
                source = kv.at[s, 2 * sub + direction]
                ring_copy(direction, 2 * s - 2 + sub, source).wait_recv()
                if forward:
                    ring_copy(direction, 2 * s + 2 + sub, source).start()
        to_sibling(s).start()
        to_sibling(s - 1).wait_recv()

    def stage_kv(slot, s):
        for sub in range(2):
            for direction in range(2):
                j = 2 * sub + direction
                stage(slot + j, kv[s, j], token_base(s, sub, direction, sec))

    def stage_kvs(slot, s):
        for sub in range(2):
            for direction in range(2):
                j = 2 * sub + direction
                stage(slot + j, kvs[s, j], token_base(s, sub, direction, 1 - sec))

    def attend_all():
        for i in range(2):
            for r in range(tiles):
                attend(i, r, 0, 8)

    arrivals(1, True)
    stage_kv(0, 1)
    for j in range(4):
        stage(4 + j, kvs[0, j], own_base(j, 1 - sec))
    attend_all()

    def forwarding(s, carry):
        arrivals(s, True)
        stage_kv(0, s)
        stage_kvs(4, s - 1)
        attend_all()
        return carry

    lax.fori_loop(2, 6, forwarding, 0)
    arrivals(6, False)
    stage_kv(0, 6)
    stage_kvs(4, 5)
    attend_all()

    arrivals(7, False)
    stage_kv(0, 7)
    stage_kvs(4, 6)
    for r in range(tiles):
        attend(0, r, 0, 8)
    to_sibling(7).wait_recv()
    stage_kvs(8, 7)

    def o_copies(r):
        at = pl.ds(r * ROW_TILE, ROW_TILE)
        return (
            pltpu.make_async_remote_copy(
                src_ref=o_send.at[at, :], dst_ref=o_recv.at[at, :],
                send_sem=ox_sem.at[0, r], recv_sem=ox_sem.at[1, r],
                device_id=partner, device_id_type=MESH,
            ),
            pltpu.make_async_remote_copy(
                src_ref=l_send.at[r], dst_ref=l_recv.at[r],
                send_sem=ox_sem.at[2, r], recv_sem=ox_sem.at[3, r],
                device_id=partner, device_id_type=MESH,
            ),
        )

    def level(i, at):
        return m_ref[i, at, :] * SCALE + jnp.log2(acc_ref[i, at, HD:])

    for r in range(tiles):
        at = pl.ds(r * ROW_TILE, ROW_TILE)
        attend(0, r, 8, 4)
        o_send[at, :] = (acc_ref[0, at, :HD] / acc_ref[0, at, HD:]).astype(bf16)
        weight = level(0, at)
        for h in range(ROW_TILE // HD):
            l_send[r, pl.ds(8 * h, 8), :] = weight[h * HD : (h + 1) * HD].T[:8]
        for copy in o_copies(r):
            copy.start()
    for r in range(tiles):
        attend(1, r, 0, 12)
    for r in range(tiles):
        at = pl.ds(r * ROW_TILE, ROW_TILE)
        for copy in o_copies(r):
            copy.wait_recv()
        mine = level(1, at)
        theirs = jnp.concatenate(
            [
                jnp.broadcast_to(l_recv[r, 8 * h : 8 * h + 1, :], (HD, HD)).T
                for h in range(ROW_TILE // HD)
            ],
            axis=0,
        )
        top = jnp.maximum(mine, theirs)
        mine = jnp.exp2(mine - top)
        theirs = jnp.exp2(theirs - top)
        own = acc_ref[1, at, :HD] / acc_ref[1, at, HD:]
        total = (mine * own + theirs * o_recv[at, :].astype(f32)) / (mine + theirs)
        out_ref[at, :] = total.astype(bf16)

    for k in range(14):
        for direction in range(2):
            ring_copy(direction, k, kv.at[0, 0]).wait_send()
    for e in range(8):
        to_sibling(e).wait_send()
    for r in range(tiles):
        for copy in o_copies(r):
            copy.wait_send()


def body(
    projected, key_weight, value_weight, key_gain, queries, frame_tokens, span_first, span_count
):
    count, width = projected.shape
    text, sub_heads, _ = queries.shape
    rows = text * sub_heads
    part = count // 4
    steps = width // DEPTH
    out = pl.pallas_call(
        kernel,
        out_shape=jax.ShapeDtypeStruct((rows, HD), bf16),
        in_specs=[pl.BlockSpec(memory_space=pltpu.HBM)] * 8,
        out_specs=pl.BlockSpec(memory_space=pltpu.VMEM),
        scratch_shapes=[
            pltpu.VMEM((1, HD), f32),
            pltpu.SMEM((FRAMES,), jnp.int32),
            pltpu.VMEM((span_first.shape[0] // text, text), jnp.int32),
            pltpu.VMEM((span_first.shape[0] // text, text), jnp.int32),
            pltpu.VMEM((2, steps, 2 * part, DEPTH), bf16),
            pltpu.VMEM((steps, DEPTH, 2 * HD), bf16),
            pltpu.VMEM((8, 4, part, 2 * HD), bf16),
            pltpu.VMEM((8, 4, part, 2 * HD), bf16),
            pltpu.VMEM((2, rows, HD), bf16),
            pltpu.VMEM((2, rows, HD), bf16),
            pltpu.VMEM((12 * part, 2 * HD), bf16),
            pltpu.VMEM((12 * part, 2 * HD), bf16),
            pltpu.VMEM((2, rows, HD), f32),
            pltpu.VMEM((2, rows, 2 * HD), f32),
            pltpu.VMEM((rows, HD), bf16),
            pltpu.VMEM((rows, HD), bf16),
            pltpu.VMEM((rows // ROW_TILE, 8 * (ROW_TILE // HD), HD), f32),
            pltpu.VMEM((rows // ROW_TILE, 8 * (ROW_TILE // HD), HD), f32),
            pltpu.SemaphoreType.DMA((4, steps)),
            pltpu.SemaphoreType.DMA((5,)),
            pltpu.SemaphoreType.DMA((2, 14)),
            pltpu.SemaphoreType.DMA((2, 14)),
            pltpu.SemaphoreType.DMA((8,)),
            pltpu.SemaphoreType.DMA((8,)),
            pltpu.SemaphoreType.DMA((2,)),
            pltpu.SemaphoreType.DMA((4, rows // ROW_TILE)),
        ],
        compiler_params=pltpu.CompilerParams(
            collective_id=0, has_side_effects=True, vmem_limit_bytes=60 * 2**20
        ),
        name="gather_attend",
    )(
        projected, key_weight, value_weight, key_gain.reshape(1, HD),
        queries.reshape(rows, HD), frame_tokens,
        span_first.reshape(-1, text), span_count.reshape(-1, text),
    )
    return out.reshape(text, sub_heads, HD)


def solution(mesh):
    placed = (
        P(("section", "blk"), None),
        P(None, "head"),
        P(None, "head"),
        P(),
        P("blk", "section", "head"),
        P(),
        P(),
        P(),
    )
    return jax.shard_map(
        body, mesh=mesh, in_specs=placed, out_specs=P("blk", "section", "head"), check_vma=False
    )
```

```python
import functools
import math

import jax
import jax.numpy as jnp
from jax import lax
from jax.experimental import pallas as pl
from jax.experimental.pallas import tpu as pltpu
from jax.sharding import PartitionSpec as P

HD = 128
FRAMES = 32
Z = 8
NEG = -1e30
SCALE = math.log2(math.e) / math.sqrt(HD)
EPS = 1e-05
ROW_TILE = 256
DEPTH = 2048
MESH = pl.DeviceIdType.MESH
f32 = jnp.float32
bf16 = jnp.bfloat16


def nt_dot(a, b):
    return lax.dot_general(a, b, (((1,), (1,)), ((), ())), preferred_element_type=f32)


def kernel(
    x_hbm, kw_hbm, vw_hbm, gain_hbm, q_hbm, frames_hbm, first_hbm, count_hbm,
    out_ref,
    gain_ref, frames_ref, first_ref, count_ref, xb, wb, raw, kv, kvs, qb, feat, ka, va, m_ref, acc_ref, o_send, o_recv, l_send, l_recv,
    in_sem, q_sem, r_send, r_recv, s_send, s_recv, qx_sem, ox_sem,
):
    steps = xb.shape[1]
    rows = qb.shape[1]
    part = kv.shape[2]
    sec = lax.axis_index("section")
    blk = lax.axis_index("blk")
    head = lax.axis_index("head")
    y_hi = blk // Z
    z = lax.rem(blk, Z)
    partner_blk = (1 - y_hi) * Z + z
    right = (sec, y_hi * Z + lax.rem(z + 1, Z), head)
    left = (sec, y_hi * Z + lax.rem(z + Z - 1, Z), head)
    partner = (sec, partner_blk, head)
    sibling = (1 - sec, blk, head)

    def weight_copies(i):
        at = pl.ds(i * DEPTH, DEPTH)
        return (
            pltpu.make_async_copy(kw_hbm.at[at, :], wb.at[i, :, pl.ds(0, HD)], in_sem.at[0, i]),
            pltpu.make_async_copy(vw_hbm.at[at, :], wb.at[i, :, pl.ds(HD, HD)], in_sem.at[1, i]),
        )

    def row_copy(c, i):
        at = pl.ds(pl.multiple_of(2 * c * part, part), 2 * part)
        return pltpu.make_async_copy(
            x_hbm.at[at, pl.ds(i * DEPTH, DEPTH)], xb.at[c, i], in_sem.at[2 + c, i]
        )

    barrier = pltpu.get_barrier_semaphore()
    for other in (right, left, partner, sibling):
        pl.semaphore_signal(barrier, inc=1, device_id=other, device_id_type=MESH)

    def start_inputs(i, carry):
        for copy in weight_copies(i):
            copy.start()
        row_copy(0, i).start()
        return carry

    def start_rest(i, carry):
        row_copy(1, i).start()
        return carry

    lax.fori_loop(0, steps, start_inputs, 0)
    own_q = pltpu.make_async_copy(q_hbm, qb.at[1], q_sem.at[0])
    own_q.start()
    small = [
        pltpu.make_async_copy(source, target, q_sem.at[1 + i])
        for i, (source, target) in enumerate(
            (
                (frames_hbm, frames_ref),
                (first_hbm, first_ref),
                (count_hbm, count_ref),
                (gain_hbm, gain_ref),
            )
        )
    ]
    for copy in small:
        copy.start()
    lax.fori_loop(0, steps, start_rest, 0)

    def ring_copy(direction, k, source):
        return pltpu.make_async_remote_copy(
            src_ref=source, dst_ref=kv.at[1 + k // 2, 2 * (k % 2) + direction],
            send_sem=r_send.at[direction, k], recv_sem=r_recv.at[direction, k],
            device_id=(right, left)[direction], device_id_type=MESH,
        )

    def to_sibling(s):
        return pltpu.make_async_remote_copy(
            src_ref=kv.at[s], dst_ref=kvs.at[s], send_sem=s_send.at[s], recv_sem=s_recv.at[s],
            device_id=sibling, device_id_type=MESH,
        )

    q_copy = pltpu.make_async_remote_copy(
        src_ref=qb.at[1], dst_ref=qb.at[0], send_sem=qx_sem.at[0], recv_sem=qx_sem.at[1],
        device_id=partner, device_id_type=MESH,
    )
    raw[...] = jnp.zeros_like(raw)

    def half(c, carry):
        def project(i, carry):
            @pl.when(c == 0)
            def _():
                for copy in weight_copies(i):
                    copy.wait()

            row_copy(c, i).wait()

            @pl.when((c == 0) & (i == steps - 1))
            def _():
                pl.semaphore_wait(barrier, 4)
                own_q.wait()
                q_copy.start()
                for copy in small:
                    copy.wait()

            at = pl.ds(pl.multiple_of(2 * c * part, part), 2 * part)
            raw[at, :] += jnp.dot(xb[c, i], wb[i], preferred_element_type=f32)
            return carry

        lax.fori_loop(0, steps, project, 0)
        for j in range(2):
            at = pl.ds(pl.multiple_of((2 * c + j) * part, part), part)
            key_raw = raw[at, :HD]
            mean_square = jnp.mean(key_raw * key_raw, axis=1, keepdims=True)
            keys = key_raw / jnp.sqrt(mean_square + EPS) * gain_ref[...]
            kv[0, 2 * c + j, :, :HD] = keys.astype(bf16)
            kv[0, 2 * c + j, :, HD:] = raw[at, HD:].astype(bf16)
            ring_copy(j, c, kv.at[0, 2 * c + j]).start()
        return carry

    lax.fori_loop(0, 2, half, 0)
    for c in range(2):
        ring_copy(0, 2 + c, kv.at[0, 2 * c + 1]).start()
        ring_copy(1, 2 + c, kv.at[0, 2 * c]).start()
    to_sibling(0).start()

    lane = lax.broadcasted_iota(jnp.int32, (1, HD), 1)
    starts = jnp.zeros((1, HD), jnp.int32)
    ends = jnp.zeros((1, HD), jnp.int32)
    for f in range(FRAMES):
        tokens = frames_ref[f]
        starts = starts + jnp.where(lane > f, tokens, 0)
        ends = ends + jnp.where(lane >= f, tokens, 0)
    ends = jnp.where(lane < FRAMES, ends, 0)
    heads_per_row = rows // first_ref.shape[1]
    text = first_ref.shape[1]
    spread = (
        lax.broadcasted_iota(jnp.int32, (rows, text), 0) // heads_per_row
        == lax.broadcasted_iota(jnp.int32, (rows, text), 1)
    ).astype(bf16)
    frame_id = lax.broadcasted_iota(jnp.int32, (HD, text), 0)
    for i, b in ((0, partner_blk), (1, blk)):
        first = first_ref[pl.ds(b, 1), :]
        end = jnp.minimum(first + count_ref[pl.ds(b, 1), :], FRAMES)
        closed = jnp.where((frame_id >= first) & (frame_id < end), 0.0, NEG).astype(bf16)
        feat[i] = nt_dot(spread, closed).astype(bf16)

    m_ref[...] = jnp.full_like(m_ref, 2 * NEG)
    acc_ref[...] = jnp.zeros_like(acc_ref)
    va[:, HD:] = jnp.ones_like(va[:, HD:])

    def token_base(s, sub, direction, section):
        hop = (s + 1) // 2
        odd = lax.rem(s + 1, 2)
        if direction == 0:
            source, quarter = lax.rem(z + Z - hop, Z), odd + 2 * sub
        else:
            source, quarter = lax.rem(z + hop, Z), 1 - odd + 2 * sub
        return (((section * 2 + y_hi) * Z + source) * 4 + quarter) * part

    def own_base(quarter, section):
        return (((section * 2 + y_hi) * Z + z) * 4 + quarter) * part

    def stage(slot, chunk, base):
        at = pl.ds(slot * part, part)
        pos = base + lax.broadcasted_iota(jnp.int32, (part, HD), 0)
        ka[at, :HD] = chunk[:, :HD]
        ka[at, HD:] = ((pos >= starts) & (pos < ends)).astype(bf16)
        va[at, :HD] = chunk[:, HD:]

    def attend(i, r, slot, count):
        at = pl.ds(r * ROW_TILE, ROW_TILE)
        q = jnp.concatenate([qb[i, at, :], feat[i, at, :]], axis=1)
        keys_at = pl.ds(slot * part, count * part)
        k_all = ka[keys_at, :]
        v_all = va[keys_at, :]
        s = nt_dot(q, k_all)
        m_old = m_ref[i, at, :]
        m_new = jnp.maximum(m_old, jnp.max(s, axis=1, keepdims=True))
        p = jnp.exp2((s - m_new[:, :1]) * SCALE).astype(bf16)
        fade = jnp.exp2((m_old - m_new) * SCALE)
        m_ref[i, at, :] = m_new
        pv = jnp.dot(p, v_all, preferred_element_type=f32)
        acc_ref[i, at, :] = acc_ref[i, at, :] * jnp.concatenate([fade, fade], axis=1) + pv

    tiles = rows // ROW_TILE
    for j in range(4):
        stage(j, kv[0, j], own_base(j, sec))
    for r in range(tiles):
        attend(1, r, 0, 4)
    q_copy.wait()
    for r in range(tiles):
        attend(0, r, 0, 4)

    def arrivals(s, forward):
        for sub in range(2):
            for direction in range(2):
                source = kv.at[s, 2 * sub + direction]
                ring_copy(direction, 2 * s - 2 + sub, source).wait_recv()
                if forward:

                    @pl.when(s <= 5)
                    def _():
                        ring_copy(direction, 2 * s + 2 + sub, source).start()

        to_sibling(s).start()
        to_sibling(s - 1).wait_recv()

    def stage_kv(slot, s):
        for sub in range(2):
            for direction in range(2):
                j = 2 * sub + direction
                stage(slot + j, kv[s, j], token_base(s, sub, direction, sec))

    def stage_kvs(slot, s):
        for sub in range(2):
            for direction in range(2):
                j = 2 * sub + direction
                stage(slot + j, kvs[s, j], token_base(s, sub, direction, 1 - sec))

    def attend_all():
        for i in range(2):
            for r in range(tiles):
                attend(i, r, 0, 8)

    arrivals(1, True)
    stage_kv(0, 1)
    for j in range(4):
        stage(4 + j, kvs[0, j], own_base(j, 1 - sec))
    attend_all()

    def forwarding(s, carry):
        arrivals(s, True)
        stage_kv(0, s)
        stage_kvs(4, s - 1)
        attend_all()
        return carry

    lax.fori_loop(2, 7, forwarding, 0)

    arrivals(7, False)
    stage_kv(0, 7)
    stage_kvs(4, 6)
    for r in range(tiles):
        attend(0, r, 0, 8)
    to_sibling(7).wait_recv()
    stage_kvs(8, 7)

    def o_copies(r):
        at = pl.ds(r * ROW_TILE, ROW_TILE)
        return (
            pltpu.make_async_remote_copy(
                src_ref=o_send.at[at, :], dst_ref=o_recv.at[at, :],
                send_sem=ox_sem.at[0, r], recv_sem=ox_sem.at[1, r],
                device_id=partner, device_id_type=MESH,
            ),
            pltpu.make_async_remote_copy(
                src_ref=l_send.at[r], dst_ref=l_recv.at[r],
                send_sem=ox_sem.at[2, r], recv_sem=ox_sem.at[3, r],
                device_id=partner, device_id_type=MESH,
            ),
        )

    def level(i, at):
        return m_ref[i, at, :] * SCALE + jnp.log2(acc_ref[i, at, HD:])

    for r in range(tiles):
        at = pl.ds(r * ROW_TILE, ROW_TILE)
        attend(0, r, 8, 4)
        o_send[at, :] = (acc_ref[0, at, :HD] / acc_ref[0, at, HD:]).astype(bf16)
        weight = level(0, at)
        for h in range(ROW_TILE // HD):
            l_send[r, pl.ds(8 * h, 8), :] = weight[h * HD : (h + 1) * HD].T[:8]
        for copy in o_copies(r):
            copy.start()
    for r in range(tiles):
        attend(1, r, 0, 12)
    for r in range(tiles):
        at = pl.ds(r * ROW_TILE, ROW_TILE)
        for copy in o_copies(r):
            copy.wait_recv()
        mine = level(1, at)
        theirs = jnp.concatenate(
            [
                jnp.broadcast_to(l_recv[r, 8 * h : 8 * h + 1, :], (HD, HD)).T
                for h in range(ROW_TILE // HD)
            ],
            axis=0,
        )
        top = jnp.maximum(mine, theirs)
        mine = jnp.exp2(mine - top)
        theirs = jnp.exp2(theirs - top)
        own = acc_ref[1, at, :HD] / acc_ref[1, at, HD:]
        total = (mine * own + theirs * o_recv[at, :].astype(f32)) / (mine + theirs)
        out_ref[at, :] = total.astype(bf16)

    for k in range(14):
        for direction in range(2):
            ring_copy(direction, k, kv.at[0, 0]).wait_send()
    for e in range(8):
        to_sibling(e).wait_send()
    for r in range(tiles):
        for copy in o_copies(r):
            copy.wait_send()


def body(
    projected, key_weight, value_weight, key_gain, queries, frame_tokens, span_first, span_count
):
    count, width = projected.shape
    text, sub_heads, _ = queries.shape
    rows = text * sub_heads
    part = count // 4
    steps = width // DEPTH
    out = pl.pallas_call(
        kernel,
        out_shape=jax.ShapeDtypeStruct((rows, HD), bf16),
        in_specs=[pl.BlockSpec(memory_space=pltpu.HBM)] * 8,
        out_specs=pl.BlockSpec(memory_space=pltpu.VMEM),
        scratch_shapes=[
            pltpu.VMEM((1, HD), f32),
            pltpu.SMEM((FRAMES,), jnp.int32),
            pltpu.VMEM((span_first.shape[0] // text, text), jnp.int32),
            pltpu.VMEM((span_first.shape[0] // text, text), jnp.int32),
            pltpu.VMEM((2, steps, 2 * part, DEPTH), bf16),
            pltpu.VMEM((steps, DEPTH, 2 * HD), bf16),
            pltpu.VMEM((count, 2 * HD), f32),
            pltpu.VMEM((8, 4, part, 2 * HD), bf16),
            pltpu.VMEM((8, 4, part, 2 * HD), bf16),
            pltpu.VMEM((2, rows, HD), bf16),
            pltpu.VMEM((2, rows, HD), bf16),
            pltpu.VMEM((12 * part, 2 * HD), bf16),
            pltpu.VMEM((12 * part, 2 * HD), bf16),
            pltpu.VMEM((2, rows, HD), f32),
            pltpu.VMEM((2, rows, 2 * HD), f32),
            pltpu.VMEM((rows, HD), bf16),
            pltpu.VMEM((rows, HD), bf16),
            pltpu.VMEM((rows // ROW_TILE, 8 * (ROW_TILE // HD), HD), f32),
            pltpu.VMEM((rows // ROW_TILE, 8 * (ROW_TILE // HD), HD), f32),
            pltpu.SemaphoreType.DMA((4, steps)),
            pltpu.SemaphoreType.DMA((5,)),
            pltpu.SemaphoreType.DMA((2, 14)),
            pltpu.SemaphoreType.DMA((2, 14)),
            pltpu.SemaphoreType.DMA((8,)),
            pltpu.SemaphoreType.DMA((8,)),
            pltpu.SemaphoreType.DMA((2,)),
            pltpu.SemaphoreType.DMA((4, rows // ROW_TILE)),
        ],
        compiler_params=pltpu.CompilerParams(
            collective_id=0, has_side_effects=True, vmem_limit_bytes=60 * 2**20
        ),
        name="gather_attend",
    )(
        projected, key_weight, value_weight, key_gain.reshape(1, HD),
        queries.reshape(rows, HD), frame_tokens,
        span_first.reshape(-1, text), span_count.reshape(-1, text),
    )
    return out.reshape(text, sub_heads, HD)


def solution(mesh):
    placed = (
        P(("section", "blk"), None),
        P(None, "head"),
        P(None, "head"),
        P(),
        P("blk", "section", "head"),
        P(),
        P(),
        P(),
    )
    return jax.shard_map(
        body, mesh=mesh, in_specs=placed, out_specs=P("blk", "section", "head"), check_vma=False
    )
```

```python
import functools
import math

import jax
import jax.numpy as jnp
from jax import lax
from jax.experimental import pallas as pl
from jax.experimental.pallas import tpu as pltpu
from jax.sharding import PartitionSpec as P

HD = 128
FRAMES = 32
Z = 8
NEG = -1e30
SCALE = math.log2(math.e) / math.sqrt(HD)
EPS = 1e-05
ROW_TILE = 256
DEPTH = 2048
MESH = pl.DeviceIdType.MESH
f32 = jnp.float32
bf16 = jnp.bfloat16


def nt_dot(a, b):
    return lax.dot_general(a, b, (((1,), (1,)), ((), ())), preferred_element_type=f32)


def kernel(
    x_hbm, kw_hbm, vw_hbm, gain_hbm, q_hbm, frames_hbm, first_hbm, count_hbm,
    out_ref,
    gain_ref, frames_ref, first_ref, count_ref, xb, wb, raw, kv, kvs, qb, feat, ka, va, m_ref, acc_ref, o_send, o_recv, l_send, l_recv,
    in_sem, q_sem, r_send, r_recv, s_send, s_recv, qx_sem, ox_sem,
):
    steps = xb.shape[1]
    rows = qb.shape[1]
    part = kv.shape[2]
    sec = lax.axis_index("section")
    blk = lax.axis_index("blk")
    head = lax.axis_index("head")
    y_hi = blk // Z
    z = lax.rem(blk, Z)
    partner_blk = (1 - y_hi) * Z + z
    right = (sec, y_hi * Z + lax.rem(z + 1, Z), head)
    left = (sec, y_hi * Z + lax.rem(z + Z - 1, Z), head)
    partner = (sec, partner_blk, head)
    sibling = (1 - sec, blk, head)

    def weight_copies(i):
        at = pl.ds(i * DEPTH, DEPTH)
        return (
            pltpu.make_async_copy(kw_hbm.at[at, :], wb.at[i, :, pl.ds(0, HD)], in_sem.at[0, i]),
            pltpu.make_async_copy(vw_hbm.at[at, :], wb.at[i, :, pl.ds(HD, HD)], in_sem.at[1, i]),
        )

    def row_copy(c, i):
        at = pl.ds(pl.multiple_of(2 * c * part, part), 2 * part)
        return pltpu.make_async_copy(
            x_hbm.at[at, pl.ds(i * DEPTH, DEPTH)], xb.at[c, i], in_sem.at[2 + c, i]
        )

    barrier = pltpu.get_barrier_semaphore()
    for other in (right, left, partner, sibling):
        pl.semaphore_signal(barrier, inc=1, device_id=other, device_id_type=MESH)

    def start_inputs(i, carry):
        for copy in weight_copies(i):
            copy.start()
        row_copy(0, i).start()
        return carry

    def start_rest(i, carry):
        row_copy(1, i).start()
        return carry

    own_q = pltpu.make_async_copy(q_hbm, qb.at[1], q_sem.at[0])
    own_q.start()
    small = [
        pltpu.make_async_copy(source, target, q_sem.at[1 + i])
        for i, (source, target) in enumerate(
            (
                (frames_hbm, frames_ref),
                (first_hbm, first_ref),
                (count_hbm, count_ref),
                (gain_hbm, gain_ref),
            )
        )
    ]
    for copy in small:
        copy.start()
    lax.fori_loop(0, steps, start_inputs, 0)
    lax.fori_loop(0, steps, start_rest, 0)

    def ring_copy(direction, k, source):
        return pltpu.make_async_remote_copy(
            src_ref=source, dst_ref=kv.at[1 + k // 2, 2 * (k % 2) + direction],
            send_sem=r_send.at[direction, k], recv_sem=r_recv.at[direction, k],
            device_id=(right, left)[direction], device_id_type=MESH,
        )

    def to_sibling(s):
        return pltpu.make_async_remote_copy(
            src_ref=kv.at[s], dst_ref=kvs.at[s], send_sem=s_send.at[s], recv_sem=s_recv.at[s],
            device_id=sibling, device_id_type=MESH,
        )

    q_copy = pltpu.make_async_remote_copy(
        src_ref=qb.at[1], dst_ref=qb.at[0], send_sem=qx_sem.at[0], recv_sem=qx_sem.at[1],
        device_id=partner, device_id_type=MESH,
    )
    def last_to_sibling(sub):
        at = pl.ds(2 * sub, 2)
        return pltpu.make_async_remote_copy(
            src_ref=kv.at[7, at], dst_ref=kvs.at[7, at],
            send_sem=s_send.at[7 + sub], recv_sem=s_recv.at[7 + sub],
            device_id=sibling, device_id_type=MESH,
        )

    raw[...] = jnp.zeros_like(raw)

    def half(c, carry):
        def project(i, carry):
            @pl.when(c == 0)
            def _():
                for copy in weight_copies(i):
                    copy.wait()

            row_copy(c, i).wait()

            @pl.when((c == 0) & (i == steps - 1))
            def _():
                pl.semaphore_wait(barrier, 4)
                own_q.wait()
                q_copy.start()
                for copy in small:
                    copy.wait()

            at = pl.ds(pl.multiple_of(2 * c * part, part), 2 * part)
            raw[at, :] += jnp.dot(xb[c, i], wb[i], preferred_element_type=f32)
            return carry

        lax.fori_loop(0, steps, project, 0)
        for j in range(2):
            at = pl.ds(pl.multiple_of((2 * c + j) * part, part), part)
            key_raw = raw[at, :HD]
            mean_square = jnp.mean(key_raw * key_raw, axis=1, keepdims=True)
            keys = key_raw / jnp.sqrt(mean_square + EPS) * gain_ref[...]
            kv[0, 2 * c + j, :, :HD] = keys.astype(bf16)
            kv[0, 2 * c + j, :, HD:] = raw[at, HD:].astype(bf16)
            ring_copy(j, c, kv.at[0, 2 * c + j]).start()
        return carry

    lax.fori_loop(0, 2, half, 0)
    for c in range(2):
        ring_copy(0, 2 + c, kv.at[0, 2 * c + 1]).start()
        ring_copy(1, 2 + c, kv.at[0, 2 * c]).start()
    to_sibling(0).start()

    lane = lax.broadcasted_iota(jnp.int32, (1, HD), 1)
    starts = jnp.zeros((1, HD), jnp.int32)
    ends = jnp.zeros((1, HD), jnp.int32)
    for f in range(FRAMES):
        tokens = frames_ref[f]
        starts = starts + jnp.where(lane > f, tokens, 0)
        ends = ends + jnp.where(lane >= f, tokens, 0)
    ends = jnp.where(lane < FRAMES, ends, 0)
    heads_per_row = rows // first_ref.shape[1]
    text = first_ref.shape[1]
    spread = (
        lax.broadcasted_iota(jnp.int32, (rows, text), 0) // heads_per_row
        == lax.broadcasted_iota(jnp.int32, (rows, text), 1)
    ).astype(bf16)
    frame_id = lax.broadcasted_iota(jnp.int32, (HD, text), 0)
    for i, b in ((0, partner_blk), (1, blk)):
        first = first_ref[pl.ds(b, 1), :]
        end = jnp.minimum(first + count_ref[pl.ds(b, 1), :], FRAMES)
        closed = jnp.where((frame_id >= first) & (frame_id < end), 0.0, NEG).astype(bf16)
        feat[i] = nt_dot(spread, closed).astype(bf16)

    m_ref[...] = jnp.full_like(m_ref, 2 * NEG)
    acc_ref[...] = jnp.zeros_like(acc_ref)
    va[:, HD:] = jnp.ones_like(va[:, HD:])

    def token_base(s, sub, direction, section):
        hop = (s + 1) // 2
        odd = lax.rem(s + 1, 2)
        if direction == 0:
            source, quarter = lax.rem(z + Z - hop, Z), odd + 2 * sub
        else:
            source, quarter = lax.rem(z + hop, Z), 1 - odd + 2 * sub
        return (((section * 2 + y_hi) * Z + source) * 4 + quarter) * part

    def own_base(quarter, section):
        return (((section * 2 + y_hi) * Z + z) * 4 + quarter) * part

    def stage(slot, chunk, base):
        at = pl.ds(slot * part, part)
        pos = base + lax.broadcasted_iota(jnp.int32, (part, HD), 0)
        ka[at, :HD] = chunk[:, :HD]
        ka[at, HD:] = ((pos >= starts) & (pos < ends)).astype(bf16)
        va[at, :HD] = chunk[:, HD:]

    def attend(i, r, slot, count):
        at = pl.ds(r * ROW_TILE, ROW_TILE)
        q = jnp.concatenate([qb[i, at, :], feat[i, at, :]], axis=1)
        keys_at = pl.ds(slot * part, count * part)
        k_all = ka[keys_at, :]
        v_all = va[keys_at, :]
        s = nt_dot(q, k_all)
        m_old = m_ref[i, at, :]
        m_new = jnp.maximum(m_old, jnp.max(s, axis=1, keepdims=True))
        p = jnp.exp2((s - m_new[:, :1]) * SCALE).astype(bf16)
        fade = jnp.exp2((m_old - m_new) * SCALE)
        m_ref[i, at, :] = m_new
        pv = jnp.dot(p, v_all, preferred_element_type=f32)
        acc_ref[i, at, :] = acc_ref[i, at, :] * jnp.concatenate([fade, fade], axis=1) + pv

    tiles = rows // ROW_TILE
    for j in range(4):
        stage(j, kv[0, j], own_base(j, sec))
    for r in range(tiles):
        attend(1, r, 0, 4)
    q_copy.wait()
    for r in range(tiles):
        attend(0, r, 0, 4)

    def arrivals(s, forward):
        for sub in range(2):
            for direction in range(2):
                source = kv.at[s, 2 * sub + direction]
                ring_copy(direction, 2 * s - 2 + sub, source).wait_recv()
                if forward:

                    @pl.when(s <= 5)
                    def _():
                        ring_copy(direction, 2 * s + 2 + sub, source).start()

        to_sibling(s).start()
        to_sibling(s - 1).wait_recv()

    def stage_kv(slot, s):
        for sub in range(2):
            for direction in range(2):
                j = 2 * sub + direction
                stage(slot + j, kv[s, j], token_base(s, sub, direction, sec))

    def stage_kvs(slot, s):
        for sub in range(2):
            for direction in range(2):
                j = 2 * sub + direction
                stage(slot + j, kvs[s, j], token_base(s, sub, direction, 1 - sec))

    def attend_all():
        for i in range(2):
            for r in range(tiles):
                attend(i, r, 0, 8)

    arrivals(1, True)
    stage_kv(0, 1)
    for j in range(4):
        stage(4 + j, kvs[0, j], own_base(j, 1 - sec))
    attend_all()

    def forwarding(s, carry):
        arrivals(s, True)
        stage_kv(0, s)
        stage_kvs(4, s - 1)
        attend_all()
        return carry

    lax.fori_loop(2, 7, forwarding, 0)

    for sub in range(2):
        for direction in range(2):
            ring_copy(direction, 12 + sub, kv.at[7, 2 * sub + direction]).wait_recv()
        last_to_sibling(sub).start()
    to_sibling(6).wait_recv()
    stage_kv(0, 7)
    stage_kvs(4, 6)
    for r in range(tiles):
        attend(0, r, 0, 8)
    for sub in range(2):
        last_to_sibling(sub).wait_recv()
    stage_kvs(8, 7)

    def o_copies(r):
        at = pl.ds(r * ROW_TILE, ROW_TILE)
        return (
            pltpu.make_async_remote_copy(
                src_ref=o_send.at[at, :], dst_ref=o_recv.at[at, :],
                send_sem=ox_sem.at[0, r], recv_sem=ox_sem.at[1, r],
                device_id=partner, device_id_type=MESH,
            ),
            pltpu.make_async_remote_copy(
                src_ref=l_send.at[r], dst_ref=l_recv.at[r],
                send_sem=ox_sem.at[2, r], recv_sem=ox_sem.at[3, r],
                device_id=partner, device_id_type=MESH,
            ),
        )

    def level(i, at):
        return m_ref[i, at, :] * SCALE + jnp.log2(acc_ref[i, at, HD:])

    for r in range(tiles):
        at = pl.ds(r * ROW_TILE, ROW_TILE)
        attend(0, r, 8, 4)
        o_send[at, :] = (acc_ref[0, at, :HD] / acc_ref[0, at, HD:]).astype(bf16)
        weight = level(0, at)
        for h in range(ROW_TILE // HD):
            l_send[r, pl.ds(8 * h, 8), :] = weight[h * HD : (h + 1) * HD].T[:8]
        for copy in o_copies(r):
            copy.start()
    for r in range(tiles):
        attend(1, r, 0, 12)
    for r in range(tiles):
        at = pl.ds(r * ROW_TILE, ROW_TILE)
        for copy in o_copies(r):
            copy.wait_recv()
        mine = level(1, at)
        theirs = jnp.concatenate(
            [
                jnp.broadcast_to(l_recv[r, 8 * h : 8 * h + 1, :], (HD, HD)).T
                for h in range(ROW_TILE // HD)
            ],
            axis=0,
        )
        top = jnp.maximum(mine, theirs)
        mine = jnp.exp2(mine - top)
        theirs = jnp.exp2(theirs - top)
        own = acc_ref[1, at, :HD] / acc_ref[1, at, HD:]
        total = (mine * own + theirs * o_recv[at, :].astype(f32)) / (mine + theirs)
        out_ref[at, :] = total.astype(bf16)

    for k in range(14):
        for direction in range(2):
            ring_copy(direction, k, kv.at[0, 0]).wait_send()
    for e in range(7):
        to_sibling(e).wait_send()
    for sub in range(2):
        last_to_sibling(sub).wait_send()
    for r in range(tiles):
        for copy in o_copies(r):
            copy.wait_send()


def body(
    projected, key_weight, value_weight, key_gain, queries, frame_tokens, span_first, span_count
):
    count, width = projected.shape
    text, sub_heads, _ = queries.shape
    rows = text * sub_heads
    part = count // 4
    steps = width // DEPTH
    out = pl.pallas_call(
        kernel,
        out_shape=jax.ShapeDtypeStruct((rows, HD), bf16),
        in_specs=[pl.BlockSpec(memory_space=pltpu.HBM)] * 8,
        out_specs=pl.BlockSpec(memory_space=pltpu.VMEM),
        scratch_shapes=[
            pltpu.VMEM((1, HD), f32),
            pltpu.SMEM((FRAMES,), jnp.int32),
            pltpu.VMEM((span_first.shape[0] // text, text), jnp.int32),
            pltpu.VMEM((span_first.shape[0] // text, text), jnp.int32),
            pltpu.VMEM((2, steps, 2 * part, DEPTH), bf16),
            pltpu.VMEM((steps, DEPTH, 2 * HD), bf16),
            pltpu.VMEM((count, 2 * HD), f32),
            pltpu.VMEM((8, 4, part, 2 * HD), bf16),
            pltpu.VMEM((8, 4, part, 2 * HD), bf16),
            pltpu.VMEM((2, rows, HD), bf16),
            pltpu.VMEM((2, rows, HD), bf16),
            pltpu.VMEM((12 * part, 2 * HD), bf16),
            pltpu.VMEM((12 * part, 2 * HD), bf16),
            pltpu.VMEM((2, rows, HD), f32),
            pltpu.VMEM((2, rows, 2 * HD), f32),
            pltpu.VMEM((rows, HD), bf16),
            pltpu.VMEM((rows, HD), bf16),
            pltpu.VMEM((rows // ROW_TILE, 8 * (ROW_TILE // HD), HD), f32),
            pltpu.VMEM((rows // ROW_TILE, 8 * (ROW_TILE // HD), HD), f32),
            pltpu.SemaphoreType.DMA((4, steps)),
            pltpu.SemaphoreType.DMA((5,)),
            pltpu.SemaphoreType.DMA((2, 14)),
            pltpu.SemaphoreType.DMA((2, 14)),
            pltpu.SemaphoreType.DMA((9,)),
            pltpu.SemaphoreType.DMA((9,)),
            pltpu.SemaphoreType.DMA((2,)),
            pltpu.SemaphoreType.DMA((4, rows // ROW_TILE)),
        ],
        compiler_params=pltpu.CompilerParams(
            collective_id=0, has_side_effects=True, vmem_limit_bytes=60 * 2**20
        ),
        name="gather_attend",
    )(
        projected, key_weight, value_weight, key_gain.reshape(1, HD),
        queries.reshape(rows, HD), frame_tokens,
        span_first.reshape(-1, text), span_count.reshape(-1, text),
    )
    return out.reshape(text, sub_heads, HD)


def solution(mesh):
    placed = (
        P(("section", "blk"), None),
        P(None, "head"),
        P(None, "head"),
        P(),
        P("blk", "section", "head"),
        P(),
        P(),
        P(),
    )
    return jax.shard_map(
        body, mesh=mesh, in_specs=placed, out_specs=P("blk", "section", "head"), check_vma=False
    )
```

```python
import functools
import math

import jax
import jax.numpy as jnp
from jax import lax
from jax.experimental import pallas as pl
from jax.experimental.pallas import tpu as pltpu
from jax.sharding import PartitionSpec as P

HD = 128
FRAMES = 32
Z = 8
NEG = -1e30
SCALE = math.log2(math.e) / math.sqrt(HD)
EPS = 1e-05
ROW_TILE = 256
DEPTH = 2048
MESH = pl.DeviceIdType.MESH
f32 = jnp.float32
bf16 = jnp.bfloat16


def nt_dot(a, b):
    return lax.dot_general(a, b, (((1,), (1,)), ((), ())), preferred_element_type=f32)


def kernel(
    x_hbm, kw_hbm, vw_hbm, gain_hbm, q_hbm, frames_hbm, first_hbm, count_hbm,
    out_ref,
    gain_ref, frames_ref, first_ref, count_ref, xb, wb, raw, kv, kvs, qb, feat, ka, va, m_ref, acc_ref, o_send, o_recv, l_send, l_recv,
    in_sem, q_sem, r_send, r_recv, s_send, s_recv, qx_sem, ox_sem,
):
    steps = xb.shape[1]
    rows = qb.shape[1]
    part = kv.shape[2]
    sec = lax.axis_index("section")
    blk = lax.axis_index("blk")
    head = lax.axis_index("head")
    y_hi = blk // Z
    z = lax.rem(blk, Z)
    partner_blk = (1 - y_hi) * Z + z
    right = (sec, y_hi * Z + lax.rem(z + 1, Z), head)
    left = (sec, y_hi * Z + lax.rem(z + Z - 1, Z), head)
    partner = (sec, partner_blk, head)
    sibling = (1 - sec, blk, head)

    def weight_copies(i):
        at = pl.ds(i * DEPTH, DEPTH)
        return (
            pltpu.make_async_copy(kw_hbm.at[at, :], wb.at[i, :, pl.ds(0, HD)], in_sem.at[0, i]),
            pltpu.make_async_copy(vw_hbm.at[at, :], wb.at[i, :, pl.ds(HD, HD)], in_sem.at[1, i]),
        )

    def row_copy(c, i):
        at = pl.ds(pl.multiple_of(2 * c * part, part), 2 * part)
        return pltpu.make_async_copy(
            x_hbm.at[at, pl.ds(i * DEPTH, DEPTH)], xb.at[c, i], in_sem.at[2 + c, i]
        )

    barrier = pltpu.get_barrier_semaphore()
    for other in (right, left, partner, sibling):
        pl.semaphore_signal(barrier, inc=1, device_id=other, device_id_type=MESH)

    def start_inputs(i, carry):
        for copy in weight_copies(i):
            copy.start()
        row_copy(0, i).start()
        return carry

    def start_rest(i, carry):
        row_copy(1, i).start()
        return carry

    own_q = pltpu.make_async_copy(q_hbm, qb.at[1], q_sem.at[0])
    own_q.start()
    small = [
        pltpu.make_async_copy(source, target, q_sem.at[1 + i])
        for i, (source, target) in enumerate(
            (
                (frames_hbm, frames_ref),
                (first_hbm, first_ref),
                (count_hbm, count_ref),
                (gain_hbm, gain_ref),
            )
        )
    ]
    for copy in small:
        copy.start()
    lax.fori_loop(0, steps, start_inputs, 0)
    lax.fori_loop(0, steps, start_rest, 0)

    def ring_copy(direction, k, source):
        return pltpu.make_async_remote_copy(
            src_ref=source, dst_ref=kv.at[1 + k // 2, 2 * (k % 2) + direction],
            send_sem=r_send.at[direction, k], recv_sem=r_recv.at[direction, k],
            device_id=(right, left)[direction], device_id_type=MESH,
        )

    def to_sibling(s):
        return pltpu.make_async_remote_copy(
            src_ref=kv.at[s], dst_ref=kvs.at[s], send_sem=s_send.at[s], recv_sem=s_recv.at[s],
            device_id=sibling, device_id_type=MESH,
        )

    q_copy = pltpu.make_async_remote_copy(
        src_ref=qb.at[1], dst_ref=qb.at[0], send_sem=qx_sem.at[0], recv_sem=qx_sem.at[1],
        device_id=partner, device_id_type=MESH,
    )
    raw[...] = jnp.zeros_like(raw)

    def half(c, carry):
        def project(i, carry):
            @pl.when(c == 0)
            def _():
                for copy in weight_copies(i):
                    copy.wait()

            row_copy(c, i).wait()

            @pl.when((c == 0) & (i == steps - 1))
            def _():
                pl.semaphore_wait(barrier, 4)
                own_q.wait()
                q_copy.start()
                for copy in small:
                    copy.wait()

            at = pl.ds(pl.multiple_of(2 * c * part, part), 2 * part)
            raw[at, :] += jnp.dot(xb[c, i], wb[i], preferred_element_type=f32)
            return carry

        lax.fori_loop(0, steps, project, 0)
        for j in range(2):
            at = pl.ds(pl.multiple_of((2 * c + j) * part, part), part)
            key_raw = raw[at, :HD]
            mean_square = jnp.mean(key_raw * key_raw, axis=1, keepdims=True)
            keys = key_raw / jnp.sqrt(mean_square + EPS) * gain_ref[...]
            slot = 2 * c + 1 - j
            kv[0, slot, :, :HD] = keys.astype(bf16)
            kv[0, slot, :, HD:] = raw[at, HD:].astype(bf16)
            ring_copy(j, c, kv.at[0, slot]).start()
        return carry

    lax.fori_loop(0, 2, half, 0)
    for c in range(2):
        ring_copy(0, 2 + c, kv.at[0, 2 * c]).start()
        ring_copy(1, 2 + c, kv.at[0, 2 * c + 1]).start()
    to_sibling(0).start()

    lane = lax.broadcasted_iota(jnp.int32, (1, HD), 1)
    starts = jnp.zeros((1, HD), jnp.int32)
    ends = jnp.zeros((1, HD), jnp.int32)
    for f in range(FRAMES):
        tokens = frames_ref[f]
        starts = starts + jnp.where(lane > f, tokens, 0)
        ends = ends + jnp.where(lane >= f, tokens, 0)
    ends = jnp.where(lane < FRAMES, ends, 0)
    heads_per_row = rows // first_ref.shape[1]
    text = first_ref.shape[1]
    spread = (
        lax.broadcasted_iota(jnp.int32, (rows, text), 0) // heads_per_row
        == lax.broadcasted_iota(jnp.int32, (rows, text), 1)
    ).astype(bf16)
    frame_id = lax.broadcasted_iota(jnp.int32, (HD, text), 0)
    for i, b in ((0, partner_blk), (1, blk)):
        first = first_ref[pl.ds(b, 1), :]
        end = jnp.minimum(first + count_ref[pl.ds(b, 1), :], FRAMES)
        closed = jnp.where((frame_id >= first) & (frame_id < end), 0.0, NEG).astype(bf16)
        feat[i] = nt_dot(spread, closed).astype(bf16)

    m_ref[...] = jnp.full_like(m_ref, 2 * NEG)
    acc_ref[...] = jnp.zeros_like(acc_ref)
    va[:, HD:] = jnp.ones_like(va[:, HD:])

    def token_base(s, sub, direction, section):
        hop = (s + 1) // 2
        odd = lax.rem(s + 1, 2)
        if direction == 0:
            source, quarter = lax.rem(z + Z - hop, Z), odd + 2 * sub
        else:
            source, quarter = lax.rem(z + hop, Z), 1 - odd + 2 * sub
        return (((section * 2 + y_hi) * Z + source) * 4 + quarter) * part

    def stage(slot, chunk, base):
        at = pl.ds(slot * part, part)
        pos = base + lax.broadcasted_iota(jnp.int32, (part, HD), 0)
        ka[at, :HD] = chunk[:, :HD]
        ka[at, HD:] = ((pos >= starts) & (pos < ends)).astype(bf16)
        va[at, :HD] = chunk[:, HD:]

    def attend(i, r, slot, count):
        at = pl.ds(r * ROW_TILE, ROW_TILE)
        q = jnp.concatenate([qb[i, at, :], feat[i, at, :]], axis=1)
        keys_at = pl.ds(slot * part, count * part)
        k_all = ka[keys_at, :]
        v_all = va[keys_at, :]
        s = nt_dot(q, k_all)
        m_old = m_ref[i, at, :]
        m_new = jnp.maximum(m_old, jnp.max(s, axis=1, keepdims=True))
        p = jnp.exp2((s - m_new[:, :1]) * SCALE).astype(bf16)
        fade = jnp.exp2((m_old - m_new) * SCALE)
        m_ref[i, at, :] = m_new
        pv = jnp.dot(p, v_all, preferred_element_type=f32)
        acc_ref[i, at, :] = acc_ref[i, at, :] * jnp.concatenate([fade, fade], axis=1) + pv

    tiles = rows // ROW_TILE
    def arrivals(s):
        for sub in range(2):
            for direction in range(2):
                source = kv.at[s, 2 * sub + direction]
                ring_copy(direction, 2 * s - 2 + sub, source).wait_recv()

                @pl.when(s <= 5)
                def _():
                    ring_copy(direction, 2 * s + 2 + sub, source).start()

        to_sibling(s).start()
        to_sibling(s - 1).wait_recv()

    def stage_kv(slot, s):
        for sub in range(2):
            for direction in range(2):
                j = 2 * sub + direction
                stage(slot + j, kv[s, j], token_base(s, sub, direction, sec))

    def stage_kvs(slot, s):
        for sub in range(2):
            for direction in range(2):
                j = 2 * sub + direction
                stage(slot + j, kvs[s, j], token_base(s, sub, direction, 1 - sec))

    def attend_all():
        for i in range(2):
            for r in range(tiles):
                attend(i, r, 0, 8)

    stage_kv(0, 0)
    for r in range(tiles):
        attend(1, r, 0, 4)
    arrivals(1)
    q_copy.wait()
    for r in range(tiles):
        attend(0, r, 0, 4)

    def turn(s, carry):
        stage_kv(0, s)
        stage_kvs(4, s - 1)
        attend_all()
        arrivals(s + 1)
        return carry

    lax.fori_loop(1, 7, turn, 0)

    stage_kv(0, 7)
    stage_kvs(4, 6)
    for r in range(tiles):
        attend(0, r, 0, 8)
    to_sibling(7).wait_recv()
    stage_kvs(8, 7)

    def o_copies(r):
        at = pl.ds(r * ROW_TILE, ROW_TILE)
        return (
            pltpu.make_async_remote_copy(
                src_ref=o_send.at[at, :], dst_ref=o_recv.at[at, :],
                send_sem=ox_sem.at[0, r], recv_sem=ox_sem.at[1, r],
                device_id=partner, device_id_type=MESH,
            ),
            pltpu.make_async_remote_copy(
                src_ref=l_send.at[r], dst_ref=l_recv.at[r],
                send_sem=ox_sem.at[2, r], recv_sem=ox_sem.at[3, r],
                device_id=partner, device_id_type=MESH,
            ),
        )

    def level(i, at):
        return m_ref[i, at, :] * SCALE + jnp.log2(acc_ref[i, at, HD:])

    for r in range(tiles):
        at = pl.ds(r * ROW_TILE, ROW_TILE)
        attend(0, r, 8, 4)
        o_send[at, :] = (acc_ref[0, at, :HD] / acc_ref[0, at, HD:]).astype(bf16)
        weight = level(0, at)
        for h in range(ROW_TILE // HD):
            l_send[r, pl.ds(8 * h, 8), :] = weight[h * HD : (h + 1) * HD].T[:8]
        for copy in o_copies(r):
            copy.start()
    for r in range(tiles):
        attend(1, r, 0, 12)
    for r in range(tiles):
        at = pl.ds(r * ROW_TILE, ROW_TILE)
        for copy in o_copies(r):
            copy.wait_recv()
        mine = level(1, at)
        theirs = jnp.concatenate(
            [
                jnp.broadcast_to(l_recv[r, 8 * h : 8 * h + 1, :], (HD, HD)).T
                for h in range(ROW_TILE // HD)
            ],
            axis=0,
        )
        top = jnp.maximum(mine, theirs)
        mine = jnp.exp2(mine - top)
        theirs = jnp.exp2(theirs - top)
        own = acc_ref[1, at, :HD] / acc_ref[1, at, HD:]
        total = (mine * own + theirs * o_recv[at, :].astype(f32)) / (mine + theirs)
        out_ref[at, :] = total.astype(bf16)

    for k in range(14):
        for direction in range(2):
            ring_copy(direction, k, kv.at[0, 0]).wait_send()
    for e in range(8):
        to_sibling(e).wait_send()
    for r in range(tiles):
        for copy in o_copies(r):
            copy.wait_send()


def body(
    projected, key_weight, value_weight, key_gain, queries, frame_tokens, span_first, span_count
):
    count, width = projected.shape
    text, sub_heads, _ = queries.shape
    rows = text * sub_heads
    part = count // 4
    steps = width // DEPTH
    out = pl.pallas_call(
        kernel,
        out_shape=jax.ShapeDtypeStruct((rows, HD), bf16),
        in_specs=[pl.BlockSpec(memory_space=pltpu.HBM)] * 8,
        out_specs=pl.BlockSpec(memory_space=pltpu.VMEM),
        scratch_shapes=[
            pltpu.VMEM((1, HD), f32),
            pltpu.SMEM((FRAMES,), jnp.int32),
            pltpu.VMEM((span_first.shape[0] // text, text), jnp.int32),
            pltpu.VMEM((span_first.shape[0] // text, text), jnp.int32),
            pltpu.VMEM((2, steps, 2 * part, DEPTH), bf16),
            pltpu.VMEM((steps, DEPTH, 2 * HD), bf16),
            pltpu.VMEM((count, 2 * HD), f32),
            pltpu.VMEM((8, 4, part, 2 * HD), bf16),
            pltpu.VMEM((8, 4, part, 2 * HD), bf16),
            pltpu.VMEM((2, rows, HD), bf16),
            pltpu.VMEM((2, rows, HD), bf16),
            pltpu.VMEM((12 * part, 2 * HD), bf16),
            pltpu.VMEM((12 * part, 2 * HD), bf16),
            pltpu.VMEM((2, rows, HD), f32),
            pltpu.VMEM((2, rows, 2 * HD), f32),
            pltpu.VMEM((rows, HD), bf16),
            pltpu.VMEM((rows, HD), bf16),
            pltpu.VMEM((rows // ROW_TILE, 8 * (ROW_TILE // HD), HD), f32),
            pltpu.VMEM((rows // ROW_TILE, 8 * (ROW_TILE // HD), HD), f32),
            pltpu.SemaphoreType.DMA((4, steps)),
            pltpu.SemaphoreType.DMA((5,)),
            pltpu.SemaphoreType.DMA((2, 14)),
            pltpu.SemaphoreType.DMA((2, 14)),
            pltpu.SemaphoreType.DMA((8,)),
            pltpu.SemaphoreType.DMA((8,)),
            pltpu.SemaphoreType.DMA((2,)),
            pltpu.SemaphoreType.DMA((4, rows // ROW_TILE)),
        ],
        compiler_params=pltpu.CompilerParams(
            collective_id=0, has_side_effects=True, vmem_limit_bytes=60 * 2**20
        ),
        name="gather_attend",
    )(
        projected, key_weight, value_weight, key_gain.reshape(1, HD),
        queries.reshape(rows, HD), frame_tokens,
        span_first.reshape(-1, text), span_count.reshape(-1, text),
    )
    return out.reshape(text, sub_heads, HD)


def solution(mesh):
    placed = (
        P(("section", "blk"), None),
        P(None, "head"),
        P(None, "head"),
        P(),
        P("blk", "section", "head"),
        P(),
        P(),
        P(),
    )
    return jax.shard_map(
        body, mesh=mesh, in_specs=placed, out_specs=P("blk", "section", "head"), check_vma=False
    )
```

```python
import functools
import math

import jax
import jax.numpy as jnp
from jax import lax
from jax.experimental import pallas as pl
from jax.experimental.pallas import tpu as pltpu
from jax.sharding import PartitionSpec as P

HD = 128
FRAMES = 32
Z = 8
NEG = -1e30
SCALE = math.log2(math.e) / math.sqrt(HD)
EPS = 1e-05
ROW_TILE = 256
DEPTH = 2048
MESH = pl.DeviceIdType.MESH
f32 = jnp.float32
bf16 = jnp.bfloat16


def nt_dot(a, b):
    return lax.dot_general(a, b, (((1,), (1,)), ((), ())), preferred_element_type=f32)


def kernel(
    x_hbm, kw_hbm, vw_hbm, gain_hbm, q_hbm, frames_hbm, first_hbm, count_hbm,
    out_ref,
    gain_ref, frames_ref, first_ref, count_ref, xb, wb, raw, kv, kvs, qb, feat, ka, va, m_ref, acc_ref, o_send, o_recv, l_send, l_recv,
    in_sem, q_sem, r_send, r_recv, s_send, s_recv, qx_sem, ox_sem,
):
    steps = xb.shape[1]
    rows = qb.shape[1]
    part = kv.shape[2]
    sec = lax.axis_index("section")
    blk = lax.axis_index("blk")
    head = lax.axis_index("head")
    y_hi = blk // Z
    z = lax.rem(blk, Z)
    partner_blk = (1 - y_hi) * Z + z
    right = (sec, y_hi * Z + lax.rem(z + 1, Z), head)
    left = (sec, y_hi * Z + lax.rem(z + Z - 1, Z), head)
    partner = (sec, partner_blk, head)
    sibling = (1 - sec, blk, head)

    def weight_copies(i):
        at = pl.ds(i * DEPTH, DEPTH)
        return (
            pltpu.make_async_copy(kw_hbm.at[at, :], wb.at[i, :, pl.ds(0, HD)], in_sem.at[0, i]),
            pltpu.make_async_copy(vw_hbm.at[at, :], wb.at[i, :, pl.ds(HD, HD)], in_sem.at[1, i]),
        )

    def row_copy(c, i):
        at = pl.ds(pl.multiple_of(2 * c * part, part), 2 * part)
        return pltpu.make_async_copy(
            x_hbm.at[at, pl.ds(i * DEPTH, DEPTH)], xb.at[c, i], in_sem.at[2 + c, i]
        )

    barrier = pltpu.get_barrier_semaphore()
    for other in (right, left, partner, sibling):
        pl.semaphore_signal(barrier, inc=1, device_id=other, device_id_type=MESH)

    def start_inputs(i, carry):
        for copy in weight_copies(i):
            copy.start()
        row_copy(0, i).start()
        return carry

    def start_rest(i, carry):
        row_copy(1, i).start()
        return carry

    own_q = pltpu.make_async_copy(q_hbm, qb.at[1], q_sem.at[0])
    own_q.start()
    small = [
        pltpu.make_async_copy(source, target, q_sem.at[1 + i])
        for i, (source, target) in enumerate(
            (
                (frames_hbm, frames_ref),
                (first_hbm, first_ref),
                (count_hbm, count_ref),
                (gain_hbm, gain_ref),
            )
        )
    ]
    for copy in small:
        copy.start()
    lax.fori_loop(0, steps, start_inputs, 0)
    lax.fori_loop(0, steps, start_rest, 0)

    def ring_copy(direction, k, source):
        return pltpu.make_async_remote_copy(
            src_ref=source, dst_ref=kv.at[1 + k // 2, 2 * (k % 2) + direction],
            send_sem=r_send.at[direction, k], recv_sem=r_recv.at[direction, k],
            device_id=(right, left)[direction], device_id_type=MESH,
        )

    def to_sibling(s, sub):
        at = pl.ds(2 * sub, 2)
        return pltpu.make_async_remote_copy(
            src_ref=kv.at[s, at], dst_ref=kvs.at[s, at],
            send_sem=s_send.at[s, sub], recv_sem=s_recv.at[s, sub],
            device_id=sibling, device_id_type=MESH,
        )

    q_copy = pltpu.make_async_remote_copy(
        src_ref=qb.at[1], dst_ref=qb.at[0], send_sem=qx_sem.at[0], recv_sem=qx_sem.at[1],
        device_id=partner, device_id_type=MESH,
    )
    raw[...] = jnp.zeros_like(raw)

    def half(c, carry):
        def project(i, carry):
            @pl.when(c == 0)
            def _():
                for copy in weight_copies(i):
                    copy.wait()

            row_copy(c, i).wait()

            @pl.when((c == 0) & (i == steps - 1))
            def _():
                pl.semaphore_wait(barrier, 4)
                own_q.wait()
                q_copy.start()
                for copy in small:
                    copy.wait()

            at = pl.ds(pl.multiple_of(2 * c * part, part), 2 * part)
            raw[at, :] += jnp.dot(xb[c, i], wb[i], preferred_element_type=f32)
            return carry

        lax.fori_loop(0, steps, project, 0)
        for j in range(2):
            at = pl.ds(pl.multiple_of((2 * c + j) * part, part), part)
            key_raw = raw[at, :HD]
            mean_square = jnp.mean(key_raw * key_raw, axis=1, keepdims=True)
            keys = key_raw / jnp.sqrt(mean_square + EPS) * gain_ref[...]
            slot = 2 * c + 1 - j
            kv[0, slot, :, :HD] = keys.astype(bf16)
            kv[0, slot, :, HD:] = raw[at, HD:].astype(bf16)
            ring_copy(j, c, kv.at[0, slot]).start()
        return carry

    lax.fori_loop(0, 2, half, 0)
    for c in range(2):
        ring_copy(0, 2 + c, kv.at[0, 2 * c]).start()
        ring_copy(1, 2 + c, kv.at[0, 2 * c + 1]).start()
    for sub in range(2):
        to_sibling(0, sub).start()

    lane = lax.broadcasted_iota(jnp.int32, (1, HD), 1)
    starts = jnp.zeros((1, HD), jnp.int32)
    ends = jnp.zeros((1, HD), jnp.int32)
    for f in range(FRAMES):
        tokens = frames_ref[f]
        starts = starts + jnp.where(lane > f, tokens, 0)
        ends = ends + jnp.where(lane >= f, tokens, 0)
    ends = jnp.where(lane < FRAMES, ends, 0)
    heads_per_row = rows // first_ref.shape[1]
    text = first_ref.shape[1]
    spread = (
        lax.broadcasted_iota(jnp.int32, (rows, text), 0) // heads_per_row
        == lax.broadcasted_iota(jnp.int32, (rows, text), 1)
    ).astype(bf16)
    frame_id = lax.broadcasted_iota(jnp.int32, (HD, text), 0)
    for i, b in ((0, partner_blk), (1, blk)):
        first = first_ref[pl.ds(b, 1), :]
        end = jnp.minimum(first + count_ref[pl.ds(b, 1), :], FRAMES)
        closed = jnp.where((frame_id >= first) & (frame_id < end), 0.0, NEG).astype(bf16)
        feat[i] = nt_dot(spread, closed).astype(bf16)

    m_ref[...] = jnp.full_like(m_ref, 2 * NEG)
    acc_ref[...] = jnp.zeros_like(acc_ref)
    va[:, HD:] = jnp.ones_like(va[:, HD:])

    def token_base(s, sub, direction, section):
        hop = (s + 1) // 2
        odd = lax.rem(s + 1, 2)
        if direction == 0:
            source, quarter = lax.rem(z + Z - hop, Z), odd + 2 * sub
        else:
            source, quarter = lax.rem(z + hop, Z), 1 - odd + 2 * sub
        return (((section * 2 + y_hi) * Z + source) * 4 + quarter) * part

    def stage(slot, chunk, base):
        at = pl.ds(slot * part, part)
        pos = base + lax.broadcasted_iota(jnp.int32, (part, HD), 0)
        ka[at, :HD] = chunk[:, :HD]
        ka[at, HD:] = ((pos >= starts) & (pos < ends)).astype(bf16)
        va[at, :HD] = chunk[:, HD:]

    def attend(i, r, slot, count):
        at = pl.ds(r * ROW_TILE, ROW_TILE)
        q = jnp.concatenate([qb[i, at, :], feat[i, at, :]], axis=1)
        keys_at = pl.ds(slot * part, count * part)
        k_all = ka[keys_at, :]
        v_all = va[keys_at, :]
        s = nt_dot(q, k_all)
        m_old = m_ref[i, at, :]
        m_new = jnp.maximum(m_old, jnp.max(s, axis=1, keepdims=True))
        p = jnp.exp2((s - m_new[:, :1]) * SCALE).astype(bf16)
        fade = jnp.exp2((m_old - m_new) * SCALE)
        m_ref[i, at, :] = m_new
        pv = jnp.dot(p, v_all, preferred_element_type=f32)
        acc_ref[i, at, :] = acc_ref[i, at, :] * jnp.concatenate([fade, fade], axis=1) + pv

    tiles = rows // ROW_TILE

    def arrivals(s):
        for sub in range(2):
            for direction in range(2):
                source = kv.at[s, 2 * sub + direction]
                ring_copy(direction, 2 * s - 2 + sub, source).wait_recv()

                @pl.when(s <= 5)
                def _():
                    ring_copy(direction, 2 * s + 2 + sub, source).start()

            to_sibling(s, sub).start()
        for sub in range(2):
            to_sibling(s - 1, sub).wait_recv()

    def stage_kv(slot, s):
        for sub in range(2):
            for direction in range(2):
                j = 2 * sub + direction
                stage(slot + j, kv[s, j], token_base(s, sub, direction, sec))

    def stage_kvs(slot, s):
        for sub in range(2):
            for direction in range(2):
                j = 2 * sub + direction
                stage(slot + j, kvs[s, j], token_base(s, sub, direction, 1 - sec))

    def attend_all():
        for i in range(2):
            for r in range(tiles):
                attend(i, r, 0, 8)

    stage_kv(0, 0)
    for r in range(tiles):
        attend(1, r, 0, 4)
    arrivals(1)
    q_copy.wait()
    for r in range(tiles):
        attend(0, r, 0, 4)

    def turn(s, carry):
        stage_kv(0, s)
        stage_kvs(4, s - 1)
        attend_all()
        arrivals(s + 1)
        return carry

    lax.fori_loop(1, 7, turn, 0)

    stage_kv(0, 7)
    stage_kvs(4, 6)
    for r in range(tiles):
        attend(0, r, 0, 8)
    for sub in range(2):
        to_sibling(7, sub).wait_recv()
    stage_kvs(8, 7)

    def o_copies(r):
        at = pl.ds(r * ROW_TILE, ROW_TILE)
        return (
            pltpu.make_async_remote_copy(
                src_ref=o_send.at[at, :], dst_ref=o_recv.at[at, :],
                send_sem=ox_sem.at[0, r], recv_sem=ox_sem.at[1, r],
                device_id=partner, device_id_type=MESH,
            ),
            pltpu.make_async_remote_copy(
                src_ref=l_send.at[r], dst_ref=l_recv.at[r],
                send_sem=ox_sem.at[2, r], recv_sem=ox_sem.at[3, r],
                device_id=partner, device_id_type=MESH,
            ),
        )

    def level(i, at):
        return m_ref[i, at, :] * SCALE + jnp.log2(acc_ref[i, at, HD:])

    for r in range(tiles):
        at = pl.ds(r * ROW_TILE, ROW_TILE)
        attend(0, r, 8, 4)
        o_send[at, :] = (acc_ref[0, at, :HD] / acc_ref[0, at, HD:]).astype(bf16)
        weight = level(0, at)
        for h in range(ROW_TILE // HD):
            l_send[r, pl.ds(8 * h, 8), :] = weight[h * HD : (h + 1) * HD].T[:8]
        for copy in o_copies(r):
            copy.start()
    for r in range(tiles):
        attend(1, r, 0, 12)
    for r in range(tiles):
        at = pl.ds(r * ROW_TILE, ROW_TILE)
        for copy in o_copies(r):
            copy.wait_recv()
        mine = level(1, at)
        theirs = jnp.concatenate(
            [
                jnp.broadcast_to(l_recv[r, 8 * h : 8 * h + 1, :], (HD, HD)).T
                for h in range(ROW_TILE // HD)
            ],
            axis=0,
        )
        top = jnp.maximum(mine, theirs)
        mine = jnp.exp2(mine - top)
        theirs = jnp.exp2(theirs - top)
        own = acc_ref[1, at, :HD] / acc_ref[1, at, HD:]
        total = (mine * own + theirs * o_recv[at, :].astype(f32)) / (mine + theirs)
        out_ref[at, :] = total.astype(bf16)

    for k in range(14):
        for direction in range(2):
            ring_copy(direction, k, kv.at[0, 0]).wait_send()
    for e in range(8):
        for sub in range(2):
            to_sibling(e, sub).wait_send()
    for r in range(tiles):
        for copy in o_copies(r):
            copy.wait_send()


def body(
    projected, key_weight, value_weight, key_gain, queries, frame_tokens, span_first, span_count
):
    count, width = projected.shape
    text, sub_heads, _ = queries.shape
    rows = text * sub_heads
    part = count // 4
    steps = width // DEPTH
    out = pl.pallas_call(
        kernel,
        out_shape=jax.ShapeDtypeStruct((rows, HD), bf16),
        in_specs=[pl.BlockSpec(memory_space=pltpu.HBM)] * 8,
        out_specs=pl.BlockSpec(memory_space=pltpu.VMEM),
        scratch_shapes=[
            pltpu.VMEM((1, HD), f32),
            pltpu.SMEM((FRAMES,), jnp.int32),
            pltpu.VMEM((span_first.shape[0] // text, text), jnp.int32),
            pltpu.VMEM((span_first.shape[0] // text, text), jnp.int32),
            pltpu.VMEM((2, steps, 2 * part, DEPTH), bf16),
            pltpu.VMEM((steps, DEPTH, 2 * HD), bf16),
            pltpu.VMEM((count, 2 * HD), f32),
            pltpu.VMEM((8, 4, part, 2 * HD), bf16),
            pltpu.VMEM((8, 4, part, 2 * HD), bf16),
            pltpu.VMEM((2, rows, HD), bf16),
            pltpu.VMEM((2, rows, HD), bf16),
            pltpu.VMEM((12 * part, 2 * HD), bf16),
            pltpu.VMEM((12 * part, 2 * HD), bf16),
            pltpu.VMEM((2, rows, HD), f32),
            pltpu.VMEM((2, rows, 2 * HD), f32),
            pltpu.VMEM((rows, HD), bf16),
            pltpu.VMEM((rows, HD), bf16),
            pltpu.VMEM((rows // ROW_TILE, 8 * (ROW_TILE // HD), HD), f32),
            pltpu.VMEM((rows // ROW_TILE, 8 * (ROW_TILE // HD), HD), f32),
            pltpu.SemaphoreType.DMA((4, steps)),
            pltpu.SemaphoreType.DMA((5,)),
            pltpu.SemaphoreType.DMA((2, 14)),
            pltpu.SemaphoreType.DMA((2, 14)),
            pltpu.SemaphoreType.DMA((8, 2)),
            pltpu.SemaphoreType.DMA((8, 2)),
            pltpu.SemaphoreType.DMA((2,)),
            pltpu.SemaphoreType.DMA((4, rows // ROW_TILE)),
        ],
        compiler_params=pltpu.CompilerParams(
            collective_id=0, has_side_effects=True, vmem_limit_bytes=60 * 2**20
        ),
        name="gather_attend",
    )(
        projected, key_weight, value_weight, key_gain.reshape(1, HD),
        queries.reshape(rows, HD), frame_tokens,
        span_first.reshape(-1, text), span_count.reshape(-1, text),
    )
    return out.reshape(text, sub_heads, HD)


def solution(mesh):
    placed = (
        P(("section", "blk"), None),
        P(None, "head"),
        P(None, "head"),
        P(),
        P("blk", "section", "head"),
        P(),
        P(),
        P(),
    )
    return jax.shard_map(
        body, mesh=mesh, in_specs=placed, out_specs=P("blk", "section", "head"), check_vma=False
    )
```
